128 devices in a mesh: gx: 4 (over x), gy: 2 (over core), gz: 16 (over z, y).
Axes of the slice: x: 4, y: 4, z: 4, core: 2. Of those that a mesh axis runs over, the one named last changes fastest.
Arguments:
- x_in: bfloat16 [64, 256, 6144], P(('gy', 'gz'), None, 'gx'), may hold values from -64 to 64, as said below
- ln_gain: float32 [6144], P('gx'), may hold values from 0.25 to 1.75
- w_qkv: bfloat16 [6144, 24, 3, 128], P('gx', 'gy'), may hold values from -0.078125 to 0.078125
- q_gain: float32 [128], replicated, may hold values from 0.25 to 1.75
- k_gain: float32 [128], replicated, may hold values from 0.25 to 1.75
- w_out: bfloat16 [24, 128, 6144], P('gy', None, 'gx'), may hold values from -1.5 to 1.5
- counts: int32 [64, 8], P(('gy', 'gz')), may hold values from 1 to 64, 256 in all within a row
- dest: int32 [64, 8], P(('gy', 'gz')), may hold values from 0 to 15, as said below
Outputs:
- routed: bfloat16 [2, 16, 16, 1, 64, 6144], P('gy', 'gz', None, None, None, 'gx')
The draws below stay inside these ranges and needn't reach their ends.
Inputs may be any that keep to these rules, and one draw needn't show every extreme that they name: x_in is of order one with row and feature scales of a factor up to ten. The 8 counts of an image sum to 256; the largest of them is exactly 64. `dest`: an image's 8 pieces go to different ranks; among the 2 images of one device (aligned blocks of rows) every rank is named exactly 1 times.
All inputs are finite; a program needn't handle non-finite values.
Results may differ from the reference program's by a relative error of at most 0.025.
Values may be sent and summed in bfloat16 or wider, within the bound.
A program may use at most 128 MiB of HBM per device.

```python
import math
import jax
import jax.numpy as jnp
import numpy as np
from jax import lax

D = 6144
HEADS = 24
HEAD_DIM = 128
PATCHES = 256
IMG_DEV = 2
PIECES = 8
IMAGES = 64
CAP = 64
ROUTE_MOST = 1
N_GX = 4
N_GY = 2
N_GZ = 16


def draw_x_in(key, part):
    key = jax.random.fold_in(key, 11)
    key_base, key_row, key_col = jax.random.split(key, 3)
    shape = (IMAGES, PATCHES, D)
    ramp = jnp.arange(D, dtype=jnp.float32) / (D - 1) - 0.5
    col_scale = 10.0 ** (jax.random.uniform(key_col, (D,), jnp.float32) - 0.5)
    row_scale = 10.0 ** (jax.random.uniform(key_row, (IMAGES, PATCHES, 1), jnp.float32) - 0.5)
    base = jnp.clip(jax.random.normal(key_base, shape, jnp.float32), -5.0, 5.0)
    trend = 3.0 ** (0.5 * ramp)
    return (0.5 * base * row_scale * col_scale * trend).astype(jnp.bfloat16)


def draw_dest(key, part):
    key = jax.random.fold_in(key, 23)
    blocks = IMAGES // IMG_DEV
    keys = jax.random.split(key, blocks)
    perms = jax.vmap(lambda one: jax.random.permutation(one, jnp.arange(N_GZ, dtype=jnp.int32)))(keys)
    position = jnp.arange(IMG_DEV * PIECES, dtype=jnp.int32) % N_GZ
    picked = jnp.take(perms, position, axis=1)
    return picked.reshape(IMAGES, PIECES).astype(jnp.int32)


def level_of(rng, extent, cuts, least, largest):
    def one(dim, blocks):
        steps = jax.random.uniform(jax.random.fold_in(jax.random.fold_in(rng, 6), dim), (blocks,), jnp.float32, least / len(cuts), largest / len(cuts))
        return jnp.repeat(jnp.exp(steps), extent[dim] // blocks).reshape((-1,) + (1,) * (len(extent) - dim - 1))

    loudness = one(*cuts[0])
    for cut in cuts[1:]:
        loudness = loudness * one(*cut)
    return loudness


def length_profile(amount, total, bound, slope):
    portions = [(1 << 20) // math.isqrt(grade ** slope) + 1 for grade in range(2, amount + 1)]
    surplus, holding = total - bound - (amount - 1), [1] * (amount - 1)
    while surplus > 0:
        candidates = [i for i in range(amount - 1) if holding[i] < bound]
        pool, budget = sum([portions[i] for i in candidates]), surplus
        for i in candidates:
            more = min(bound - holding[i], max(1, budget * portions[i] // pool), surplus)
            holding[i] = holding[i] + more
            surplus = surplus - more
    return np.array([bound] + holding)


def uneven_parts(stream_key, count, total, bound, lean):
    if count == 2:
        one = jax.random.randint(stream_key, (), max(1, total - bound), min(bound, total - 1) + 1)
        return jnp.stack([one, total - one])
    sizes = jnp.asarray(length_profile(count, total, bound, lean), jnp.int32)
    twos = (count - 1) // 2
    donor, receiver = sizes[1:1 + 2 * twos:2], sizes[2:2 + 2 * twos:2]
    margin = jnp.minimum(donor - 1, bound - receiver)
    moved = jax.random.randint(jax.random.fold_in(stream_key, 1), (twos,), 0, 1 << 20) % (margin + 1)
    sizes = sizes.at[1:1 + 2 * twos:2].set(donor - moved).at[2:2 + 2 * twos:2].set(receiver + moved)
    return sizes[jax.random.permutation(jax.random.fold_in(stream_key, 2), count)]


def scatter_about(rng, extent, spread, bound, shards=(), kind=jnp.bfloat16):
    level = level_of(rng, extent, shards, -0.22, 0.18) if shards else 1.0
    entries = jax.random.normal(rng, extent, jnp.float32) * spread * level
    return jnp.minimum(jnp.maximum(entries, -bound), bound).astype(kind)


def setup_inputs(seed: int = 0) -> dict:
    arg_keys = jax.random.split(jax.random.key(seed), 9)
    return {
        "x_in": draw_x_in(jax.random.fold_in(arg_keys[8], 71), 0),
        "ln_gain": jnp.clip(1.0 + 0.15 * jax.random.normal(arg_keys[1], (D,), jnp.float32), 0.25, 1.75),
        "w_qkv": scatter_about(arg_keys[2], (D, HEADS, 3, HEAD_DIM), D ** -0.5, 0.078125, ((0, 4), (1, 2))),
        "q_gain": jnp.clip(1.0 + 0.15 * jax.random.normal(arg_keys[3], (HEAD_DIM,), jnp.float32), 0.25, 1.75),
        "k_gain": jnp.clip(1.0 + 0.15 * jax.random.normal(arg_keys[4], (HEAD_DIM,), jnp.float32), 0.25, 1.75),
        "w_out": scatter_about(arg_keys[5], (HEADS, HEAD_DIM, D), (HEAD_DIM // 8) ** -0.5, 1.5, ((0, 2), (2, 4))),
        "counts": jax.vmap(lambda own: uneven_parts(own, PIECES, PATCHES, CAP, 1))(jax.random.split(arg_keys[6], IMAGES)).reshape((IMAGES, PIECES)).astype(jnp.int32),
        "dest": draw_dest(jax.random.fold_in(arg_keys[8], 71), 0),
    }


def layer_norm(values, gain):
    mu = lax.optimization_barrier(jnp.mean(values, axis=-1, keepdims=True))
    var = lax.optimization_barrier(jnp.mean(values * values, axis=-1, keepdims=True)) - mu * mu
    return (values - mu) * lax.rsqrt(var + 1e-06) * gain

def piece_slots(dest, counts, ranks, most, cap, patches):
    images, pieces = dest.shape
    total = images * pieces
    flat_dest = dest.reshape(total).astype(jnp.int32)
    flat_count = counts.reshape(total).astype(jnp.int32)
    offsets = (jnp.cumsum(counts, axis=1).astype(jnp.int32) - counts.astype(jnp.int32)).reshape(total)
    order = jnp.arange(total, dtype=jnp.int32)
    image_of = order // pieces
    earlier = (flat_dest[None, :] == flat_dest[:, None]) & (order[None, :] < order[:, None])
    slot = lax.optimization_barrier(jnp.sum(earlier.astype(jnp.int32), axis=1)).astype(jnp.int32)
    rank_ids = jnp.arange(ranks, dtype=jnp.int32)
    slot_ids = jnp.arange(most, dtype=jnp.int32)
    select = ((flat_dest[None, None, :] == rank_ids[:, None, None]) & (slot[None, None, :] == slot_ids[None, :, None])).astype(jnp.int32)
    first = lax.optimization_barrier(jnp.sum(select * (image_of * patches + offsets)[None, None, :], axis=2)).astype(jnp.int32)
    length = lax.optimization_barrier(jnp.sum(select * flat_count[None, None, :], axis=2)).astype(jnp.int32)
    within = jnp.arange(cap, dtype=jnp.int32)
    valid = within[None, None, :] < length[:, :, None]
    index = jnp.where(valid, first[:, :, None] + within[None, None, :], 0).astype(jnp.int32)
    return (index, valid)

def reference(x_in, ln_gain, w_qkv, q_gain, k_gain, w_out, counts, dest):
    xf = x_in.astype(jnp.float32)
    normed = layer_norm(xf, ln_gain.astype(jnp.float32)).astype(jnp.bfloat16)
    rows = normed.reshape(IMAGES * PATCHES, D)
    wmat = w_qkv.reshape(D, HEADS * 3 * HEAD_DIM)
    block = D // N_GX
    qkv = jnp.zeros((IMAGES * PATCHES, HEADS * 3 * HEAD_DIM), jnp.float32)
    for index in range(N_GX):
        part = jnp.dot(rows[:, index * block:(index + 1) * block], wmat[index * block:(index + 1) * block], preferred_element_type=jnp.float32)
        part = lax.optimization_barrier(part.astype(jnp.bfloat16)).astype(jnp.float32)
        qkv = qkv + part
    qkv = qkv.reshape(IMAGES, PATCHES, HEADS, 3, HEAD_DIM)

    def attend_image(item):
        query = layer_norm(item[:, :, 0, :], q_gain.astype(jnp.float32)).astype(jnp.bfloat16)
        keys = layer_norm(item[:, :, 1, :], k_gain.astype(jnp.float32)).astype(jnp.bfloat16)
        values = item[:, :, 2, :].astype(jnp.bfloat16)
        scores = jnp.einsum('phe,she->hps', query.astype(jnp.float32), keys.astype(jnp.float32)) / math.sqrt(HEAD_DIM)
        expo = jnp.exp(scores)
        weights = (expo / lax.optimization_barrier(jnp.sum(expo, axis=-1, keepdims=True))).astype(jnp.bfloat16)
        mixed = jnp.einsum('hps,she->phe', weights.astype(jnp.float32), values.astype(jnp.float32))
        return mixed.astype(jnp.bfloat16)
    attended = lax.map(attend_image, qkv)
    flat = attended.reshape(IMAGES * PATCHES, HEADS * HEAD_DIM)
    wo_mat = w_out.reshape(HEADS * HEAD_DIM, D)
    head_block = HEADS // N_GY * HEAD_DIM
    projected = jnp.zeros((IMAGES * PATCHES, D), jnp.float32)
    for index in range(N_GY):
        part = jnp.dot(flat[:, index * head_block:(index + 1) * head_block], wo_mat[index * head_block:(index + 1) * head_block], preferred_element_type=jnp.float32)
        part = lax.optimization_barrier(part.astype(jnp.bfloat16)).astype(jnp.float32)
        projected = projected + part
    layer_out = (xf.reshape(IMAGES * PATCHES, D) + projected).astype(jnp.bfloat16)
    blocks = N_GY * N_GZ
    block_rows = layer_out.reshape(blocks, IMG_DEV * PATCHES, D)
    block_dest = dest.reshape(blocks, IMG_DEV, PIECES)
    block_counts = counts.reshape(blocks, IMG_DEV, PIECES)

    def send(item):
        source_rows, source_dest, source_counts = item
        index, valid = piece_slots(source_dest, source_counts, N_GZ, ROUTE_MOST, CAP, PATCHES)
        picked = jnp.take(source_rows, index.reshape(-1), axis=0).reshape(N_GZ, ROUTE_MOST, CAP, D)
        return jnp.where(valid[:, :, :, None], picked, jnp.zeros((), jnp.bfloat16))
    buffers = lax.map(send, (block_rows, block_dest, block_counts))
    buffers = buffers.reshape(N_GY, N_GZ, N_GZ, ROUTE_MOST, CAP, D)
    return jnp.transpose(buffers, (0, 2, 1, 3, 4, 5))
```

```python
import functools
import math

import jax
import jax.numpy as jnp
from jax import lax
from jax.experimental import pallas as pl
from jax.experimental.pallas import tpu as pltpu
from jax.sharding import PartitionSpec as P

D = 6144
PATCHES = 256
HALF = PATCHES // 2
BLOCK = 1536
GROUP = 384
CHUNK = 3 * GROUP
RANKS = 16
CAP = 64
IMAGES = 4
EPS = 1e-06
MESH = pl.DeviceIdType.MESH
BF16 = jnp.bfloat16
F32 = jnp.float32

OPP, RIGHT, LEFT, OWN = 0, 1, 2, 3
TWO_RIGHT, TWO_LEFT, RIGHT_HIGH, LEFT_LOW, RIGHT_LOW, LEFT_HIGH = range(6)
LOW = pl.ds(0, HALF)
HIGH = pl.ds(HALF, HALF)


def head_norm(values, gain):
    mean_value = jnp.mean(values, axis=-1, keepdims=True)
    spread = jnp.mean(values * values, axis=-1, keepdims=True) - mean_value * mean_value
    return ((values - mean_value) * lax.rsqrt(spread + EPS) * gain).astype(BF16)


def kernel(
    x_hbm, gain_ref, wq_hbm, q_gain_ref, k_gain_ref, wo_hbm, counts_ref, dest_ref,
    out_hbm,
    x_ref, normed, wq, wo, two, to_right, to_left, from_two_left, from_two_right,
    from_left, from_right, own, attended, partial, other, layer, outgoing, stats, stats_in,
    x_sem, wq_sem, wo_sem, stat_send, stat_recv, norm_send, norm_recv, sum_send, sum_recv,
    att_send, att_recv, part_send, part_recv, route_send, route_recv, local_sem,
):
    gx, gy, gz = lax.axis_index("gx"), lax.axis_index("gy"), lax.axis_index("gz")
    at = {
        OPP: lax.rem(gx + 2, 4),
        RIGHT: lax.rem(gx + 1, 4),
        LEFT: lax.rem(gx + 3, 4),
        OWN: gx,
    }
    line = {role: (at[role], gy, gz) for role in (OPP, RIGHT, LEFT)}
    sibling = (gx, 1 - gy, gz)

    barrier = pltpu.get_barrier_semaphore()
    for role in (OPP, RIGHT, LEFT):
        pl.semaphore_signal(barrier, inc=1, device_id=line[role], device_id_type=MESH)
    pl.semaphore_signal(barrier, inc=1, device_id=sibling, device_id_type=MESH)
    for step in range(1, RANKS):
        pl.semaphore_signal(
            barrier, inc=1, device_id=(gx, gy, lax.rem(gz + step, RANKS)), device_id_type=MESH
        )

    x_copy = pltpu.make_async_copy(x_hbm, x_ref, x_sem)
    x_copy.start()
    wq_copies = {}
    for role in (OPP, RIGHT, LEFT, OWN):
        for k in range(9):
            wq_copies[role, k] = pltpu.make_async_copy(
                wq_hbm.at[at[role] * 3 + k // 3, k % 3],
                wq.at[role, :, pl.ds(k * 128, 128)],
                wq_sem.at[role, k],
            )
            wq_copies[role, k].start()
    wo_copies = []
    for role in (OPP, RIGHT, LEFT, OWN):
        copy = pltpu.make_async_copy(
            wo_hbm.at[pl.ds(pl.multiple_of(at[role] * GROUP, GROUP), GROUP)],
            wo.at[pl.ds(role * GROUP, GROUP)],
            wo_sem.at[role],
        )
        copy.start()
        wo_copies.append(copy)

    x_copy.wait()
    lane = lax.broadcasted_iota(jnp.int32, (PATCHES, 128), 1)
    for image in range(2):
        rows = pl.ds(image * PATCHES, PATCHES)
        xf = x_ref[rows, :].astype(F32)
        both = jnp.where(
            lane == 0,
            jnp.sum(xf, axis=-1, keepdims=True),
            jnp.sum(xf * xf, axis=-1, keepdims=True),
        )
        stats[:, rows] = jnp.transpose(both)[0:8, :]

    pl.semaphore_wait(barrier, 3 + 1 + RANKS - 1)

    mirror = {OPP: OPP, RIGHT: LEFT, LEFT: RIGHT}
    stat_copies = []
    for role in (OPP, RIGHT, LEFT):
        copy = pltpu.make_async_remote_copy(
            src_ref=stats,
            dst_ref=stats_in.at[mirror[role]],
            send_sem=stat_send.at[role],
            recv_sem=stat_recv.at[mirror[role]],
            device_id=line[role],
            device_id_type=MESH,
        )
        copy.start()
        stat_copies.append(copy)
    for copy in stat_copies:
        copy.wait()
    total = stats[...] + stats_in[0] + stats_in[1] + stats_in[2]

    def norm_copy(image):
        return pltpu.make_async_remote_copy(
            src_ref=normed.at[gy * 2 + image],
            dst_ref=normed.at[gy * 2 + image],
            send_sem=norm_send.at[image],
            recv_sem=norm_recv.at[image],
            device_id=sibling,
            device_id_type=MESH,
        )

    for image in range(2):
        rows = pl.ds(image * PATCHES, PATCHES)
        part = total[:, image * PATCHES:(image + 1) * PATCHES]
        column = jnp.transpose(jnp.concatenate([part] * 16, axis=0))
        mean_value = column[:, 0:1] * (1.0 / D)
        spread = column[:, 1:2] * (1.0 / D) - mean_value * mean_value
        scale = lax.rsqrt(spread + EPS)
        xf = x_ref[rows, :].astype(F32)
        normed[gy * 2 + image] = ((xf - mean_value) * scale * gain_ref[...]).astype(BF16)
        norm_copy(image).start()

    def sum_copy(image, kind):
        src, dst, role = {
            TWO_RIGHT: (two.at[image, LOW], from_two_left.at[image], RIGHT),
            TWO_LEFT: (two.at[image, HIGH], from_two_right.at[image], LEFT),
            RIGHT_HIGH: (to_right.at[image, HIGH], from_left.at[image, HIGH], RIGHT),
            LEFT_LOW: (to_left.at[image, LOW], from_right.at[image, LOW], LEFT),
            RIGHT_LOW: (to_right.at[image, LOW], from_left.at[image, LOW], RIGHT),
            LEFT_HIGH: (to_left.at[image, HIGH], from_right.at[image, HIGH], LEFT),
        }[kind]
        return pltpu.make_async_remote_copy(
            src_ref=src,
            dst_ref=dst,
            send_sem=sum_send.at[image, kind],
            recv_sem=sum_recv.at[image, kind],
            device_id=line[role],
            device_id_type=MESH,
        )

    def att_copy(image, role):
        return pltpu.make_async_remote_copy(
            src_ref=attended.at[image, :, pl.ds(OWN * GROUP, GROUP)],
            dst_ref=attended.at[image, :, pl.ds(mirror[role] * GROUP, GROUP)],
            send_sem=att_send.at[image, role],
            recv_sem=att_recv.at[image, mirror[role]],
            device_id=line[role],
            device_id_type=MESH,
        )

    def part_copy(image):
        slot = lax.rem(image, 2)
        return pltpu.make_async_remote_copy(
            src_ref=partial.at[image],
            dst_ref=other.at[slot],
            send_sem=part_send.at[slot],
            recv_sem=part_recv.at[slot],
            device_id=sibling,
            device_id_type=MESH,
        )

    def route_copy(step):
        return pltpu.make_async_remote_copy(
            src_ref=outgoing.at[step],
            dst_ref=out_hbm.at[gz],
            send_sem=route_send.at[step],
            recv_sem=route_recv.at[step],
            device_id=(gx, gy, lax.rem(gz + step, RANKS)),
            device_id_type=MESH,
        )

    def product(image, role):
        return jnp.dot(normed[image], wq[role], preferred_element_type=F32)

    def wait_weights(role):
        for k in range(9):
            wq_copies[role, k].wait()

    def attend(image):
        own[...] = product(image, OWN)
        for kind in (RIGHT_HIGH, LEFT_LOW, RIGHT_LOW, LEFT_HIGH):
            sum_copy(image, kind).wait_recv()
        own[...] += from_left[image].astype(F32) + from_right[image].astype(F32)
        for head in range(3):
            base = head * 384
            query = head_norm(own[:, base:base + 128], q_gain_ref[...])
            keys = head_norm(own[:, base + 128:base + 256], k_gain_ref[...])
            values = own[:, base + 256:base + 384].astype(BF16)
            scores = lax.dot_general(
                query, keys, (((1,), (1,)), ((), ())), preferred_element_type=F32
            ) * (1.0 / math.sqrt(128))
            expo = jnp.exp(scores)
            weights = (expo * (1.0 / jnp.sum(expo, axis=-1, keepdims=True))).astype(BF16)
            attended[image, :, pl.ds(OWN * GROUP + head * 128, 128)] = jnp.dot(
                weights, values, preferred_element_type=F32
            ).astype(BF16)
        for role in (OPP, RIGHT, LEFT):
            att_copy(image, role).start()

    def route():
        for image in range(2):
            part_copy(image).wait_recv()
            rows = pl.ds(image * PATCHES, PATCHES)
            layer[rows, :] = (
                x_ref[rows, :].astype(F32)
                + (partial[gy * 2 + image].astype(F32) + other[image].astype(F32))
            ).astype(BF16)
        row = lax.broadcasted_iota(jnp.int32, (1, 2 * PATCHES), 1)
        target = jnp.full((1, 2 * PATCHES), RANKS * CAP, jnp.int32)
        for image in range(2):
            start = image * PATCHES
            for piece in range(8):
                stop = start + counts_ref[image, piece]
                target = jnp.where(
                    (row >= start) & (row < stop),
                    dest_ref[image, piece] * CAP + row - start,
                    target,
                )
                start = stop
        place = lax.broadcasted_iota(jnp.int32, (4 * CAP, 1), 0)
        for quarter in range(4):
            rank = (gz + 4 * quarter + (place >> 6)) & (RANKS - 1)
            pick = jnp.where((rank * CAP + (place & (CAP - 1))) == target, 1.0, 0.0).astype(BF16)
            picked = jnp.dot(pick, layer[...], preferred_element_type=F32).astype(BF16)
            outgoing[pl.ds(4 * quarter, 4)] = picked.reshape(4, CAP, BLOCK)
            for step in range(4 * quarter, 4 * quarter + 4):
                if step == 0:
                    pltpu.make_async_copy(outgoing.at[0], out_hbm.at[gz], local_sem).start()
                else:
                    route_copy(step).start()

    def turn(step, carry):
        @pl.when((step >= 1) & (step <= IMAGES))
        def _():
            image = lax.rem(step + 3, IMAGES)

            @pl.when(step == 1)
            def _():
                wait_weights(RIGHT)
                wait_weights(LEFT)

            to_right[image] = product(image, RIGHT).astype(BF16)
            sum_copy(image, RIGHT_HIGH).start()
            to_left[image] = product(image, LEFT).astype(BF16)
            sum_copy(image, LEFT_LOW).start()

        @pl.when(step < IMAGES)
        def _():
            image = lax.rem(step, IMAGES)

            @pl.when(image // 2 != gy)
            def _():
                norm_copy(lax.rem(image, 2)).wait_recv()

            @pl.when(step == 0)
            def _():
                wait_weights(OPP)

            two[image] = product(image, OPP).astype(BF16)
            sum_copy(image, TWO_RIGHT).start()
            sum_copy(image, TWO_LEFT).start()

        @pl.when((step >= 1) & (step <= IMAGES))
        def _():
            image = lax.rem(step + 3, IMAGES)
            sum_copy(image, TWO_RIGHT).wait_recv()
            to_right[image, LOW, :] = (
                to_right[image, LOW, :].astype(F32) + from_two_left[image].astype(F32)
            ).astype(BF16)
            sum_copy(image, RIGHT_LOW).start()
            sum_copy(image, TWO_LEFT).wait_recv()
            to_left[image, HIGH, :] = (
                to_left[image, HIGH, :].astype(F32) + from_two_right[image].astype(F32)
            ).astype(BF16)
            sum_copy(image, LEFT_HIGH).start()

        @pl.when((step >= 2) & (step <= IMAGES + 1))
        def _():
            @pl.when(step == 2)
            def _():
                wait_weights(OWN)

            attend(lax.rem(step + 2, IMAGES))

        @pl.when(step >= 3)
        def _():
            image = lax.rem(step + 1, IMAGES)

            @pl.when(step == 3)
            def _():
                for copy in wo_copies:
                    copy.wait()

            for role in (OPP, RIGHT, LEFT):
                att_copy(image, role).wait_recv()
            partial[image] = jnp.dot(
                attended[image], wo[...], preferred_element_type=F32
            ).astype(BF16)

            @pl.when(image // 2 != gy)
            def _():
                part_copy(image).start()

        @pl.when(step == 4 + 2 * gy)
        def _():
            route()

        return carry

    lax.fori_loop(0, IMAGES + 3, turn, 0)

    for image in range(2):
        norm_copy(image).wait_send()
        part_copy(image).wait_send()
    for image in range(IMAGES):
        for kind in range(6):
            sum_copy(image, kind).wait_send()
        for role in (OPP, RIGHT, LEFT):
            att_copy(image, role).wait_send()
    pltpu.make_async_copy(outgoing.at[0], out_hbm.at[gz], local_sem).wait()
    for step in range(1, RANKS):
        route_copy(step).wait()


def on_device(x_in, ln_gain, w_qkv, q_gain, k_gain, w_out, counts, dest):
    any_spec = pl.BlockSpec(memory_space=pl.ANY)
    vmem_spec = pl.BlockSpec(memory_space=pltpu.VMEM)
    smem_spec = pl.BlockSpec(memory_space=pltpu.SMEM)
    dma = pltpu.SemaphoreType.DMA
    routed = pl.pallas_call(
        kernel,
        out_shape=jax.ShapeDtypeStruct((RANKS, CAP, BLOCK), BF16),
        in_specs=[
            any_spec, vmem_spec, any_spec, vmem_spec, vmem_spec, any_spec, smem_spec, smem_spec,
        ],
        out_specs=any_spec,
        scratch_shapes=[
            pltpu.VMEM((2 * PATCHES, BLOCK), BF16),
            pltpu.VMEM((IMAGES, PATCHES, BLOCK), BF16),
            pltpu.VMEM((4, BLOCK, CHUNK), BF16),
            pltpu.VMEM((BLOCK, BLOCK), BF16),
            pltpu.VMEM((IMAGES, PATCHES, CHUNK), BF16),
            pltpu.VMEM((IMAGES, PATCHES, CHUNK), BF16),
            pltpu.VMEM((IMAGES, PATCHES, CHUNK), BF16),
            pltpu.VMEM((IMAGES, HALF, CHUNK), BF16),
            pltpu.VMEM((IMAGES, HALF, CHUNK), BF16),
            pltpu.VMEM((IMAGES, PATCHES, CHUNK), BF16),
            pltpu.VMEM((IMAGES, PATCHES, CHUNK), BF16),
            pltpu.VMEM((PATCHES, CHUNK), F32),
            pltpu.VMEM((IMAGES, PATCHES, BLOCK), BF16),
            pltpu.VMEM((IMAGES, PATCHES, BLOCK), BF16),
            pltpu.VMEM((2, PATCHES, BLOCK), BF16),
            pltpu.VMEM((2 * PATCHES, BLOCK), BF16),
            pltpu.VMEM((RANKS, CAP, BLOCK), BF16),
            pltpu.VMEM((8, 2 * PATCHES), F32),
            pltpu.VMEM((3, 8, 2 * PATCHES), F32),
            dma(()),
            dma((4, 9)),
            dma((4,)),
            dma((3,)),
            dma((3,)),
            dma((2,)),
            dma((2,)),
            dma((IMAGES, 6)),
            dma((IMAGES, 6)),
            dma((IMAGES, 3)),
            dma((IMAGES, 3)),
            dma((2,)),
            dma((2,)),
            dma((RANKS,)),
            dma((RANKS,)),
            dma(()),
        ],
        compiler_params=pltpu.CompilerParams(
            collective_id=0, has_side_effects=True, vmem_limit_bytes=60 * 2**20
        ),
        cost_estimate=pl.CostEstimate(
            flops=20 * 10**9, bytes_accessed=25 * 10**6, transcendentals=10**6
        ),
        name="layer",
    )(
        x_in.reshape(2 * PATCHES, BLOCK),
        ln_gain.reshape(1, BLOCK),
        jnp.transpose(w_qkv, (1, 2, 0, 3)),
        q_gain.reshape(1, 128),
        k_gain.reshape(1, 128),
        w_out.reshape(BLOCK, BLOCK),
        counts,
        dest,
    )
    return routed.reshape(1, 1, RANKS, 1, CAP, BLOCK)


def solution(mesh):
    in_specs = (
        P(("gy", "gz"), None, "gx"),
        P("gx"),
        P("gx", "gy", None, None),
        P(),
        P(),
        P("gy", None, "gx"),
        P(("gy", "gz"), None),
        P(("gy", "gz"), None),
    )
    out_specs = P("gy", "gz", None, None, None, "gx")
    return jax.shard_map(
        on_device, mesh=mesh, in_specs=in_specs, out_specs=out_specs, check_vma=False
    )
```

```python
import functools
import math

import jax
import jax.numpy as jnp
from jax import lax
from jax.experimental import pallas as pl
from jax.experimental.pallas import tpu as pltpu
from jax.sharding import PartitionSpec as P

D = 6144
PATCHES = 256
HALF = PATCHES // 2
BLOCK = 1536
WIDE = BLOCK // 2
GROUP = 384
SLOTS = 3
RANKS = 16
RING = 4
CAP = 64
IMAGES = 4
UNITS = IMAGES * SLOTS
EPS = 1e-06
MESH = pl.DeviceIdType.MESH
BF16 = jnp.bfloat16
F32 = jnp.float32

OPP, RIGHT, LEFT, OWN = 0, 1, 2, 3
TWO_RIGHT, TWO_LEFT, RIGHT_HIGH, LEFT_LOW, RIGHT_LOW, LEFT_HIGH = range(6)
ATT_RIGHT, ATT_LEFT, PASS_RIGHT, PASS_LEFT = range(4)
LOW = pl.ds(0, HALF)
HIGH = pl.ds(HALF, HALF)


def head_norm(values, gain):
    mean_value = jnp.mean(values, axis=-1, keepdims=True)
    spread = jnp.mean(values * values, axis=-1, keepdims=True) - mean_value * mean_value
    return ((values - mean_value) * lax.rsqrt(spread + EPS) * gain).astype(BF16)


def remote(src, dst, send_sem, recv_sem, device):
    return pltpu.make_async_remote_copy(
        src_ref=src,
        dst_ref=dst,
        send_sem=send_sem,
        recv_sem=recv_sem,
        device_id=device,
        device_id_type=MESH,
    )


def kernel(
    x_hbm, gain_ref, wq_hbm, q_gain_ref, k_gain_ref, wo_hbm, counts_ref, dest_ref,
    out_hbm,
    x_ref, x_half, normed, wq, wo, two, to_right, to_left, from_two_left, from_two_right,
    from_left, from_right, attended, mine, leaving, other, layer, outgoing, middle, target,
    stats, stats_in,
    x_sem, half_sem, wq_sem, wo_sem, half_send, half_recv, target_send, target_recv,
    stat_send, stat_recv, norm_send, norm_recv, sum_send, sum_recv, att_send, att_recv,
    part_send, part_recv, first_send, first_recv, last_send, last_recv, local_sem,
):
    gx, gy, gz = lax.axis_index("gx"), lax.axis_index("gy"), lax.axis_index("gz")
    at = {
        OPP: lax.rem(gx + 2, RING),
        RIGHT: lax.rem(gx + 1, RING),
        LEFT: lax.rem(gx + 3, RING),
        OWN: gx,
    }
    line = {role: (at[role], gy, gz) for role in (OPP, RIGHT, LEFT)}
    sibling = (gx, 1 - gy, gz)
    z_at, y_at = lax.div(gz, RING), lax.rem(gz, RING)
    first_at = (1 - gy) * y_at + gy * z_at
    last_at = (1 - gy) * z_at + gy * y_at

    def plane(first, last):
        return first * (1 + 3 * gy) + last * (4 - 3 * gy)

    barrier = pltpu.get_barrier_semaphore()
    partners = [line[OPP], line[RIGHT], line[LEFT], sibling]
    for step in range(1, RING):
        for core in (gy, 1 - gy):
            partners.append((gx, core, z_at * RING + lax.rem(y_at + step, RING)))
            partners.append((gx, core, lax.rem(z_at + step, RING) * RING + y_at))
    for partner in partners:
        pl.semaphore_signal(barrier, inc=1, device_id=partner, device_id_type=MESH)

    x_copy = pltpu.make_async_copy(x_hbm, x_ref, x_sem)
    x_copy.start()

    def wq_copies(role, slot):
        return [
            pltpu.make_async_copy(
                wq_hbm.at[at[role] * SLOTS + slot, k],
                wq.at[role, slot, :, pl.ds(k * 128, 128)],
                wq_sem.at[role, slot, k],
            )
            for k in range(3)
        ]

    def wo_copies():
        for side in range(2):
            core = gy if side == 1 else 1 - gy
            for slot in range(SLOTS):
                for role in (OPP, RIGHT, LEFT, OWN):
                    row = pl.multiple_of((at[role] * SLOTS + slot) * 128, 128)
                    yield pltpu.make_async_copy(
                        wo_hbm.at[pl.ds(row, 128), pl.ds(pl.multiple_of(core * WIDE, WIDE), WIDE)],
                        wo.at[side, slot, pl.ds(role * 128, 128)],
                        wo_sem.at[side, slot, role],
                    )

    x_copy.wait()
    for slot in range(SLOTS):
        for role in (OPP, RIGHT, LEFT, OWN):
            for copy in wq_copies(role, slot):
                copy.start()
    half_copy = pltpu.make_async_copy(
        x_hbm.at[:, pl.ds(pl.multiple_of(gy * WIDE, WIDE), WIDE)], x_half.at[gy], half_sem
    )
    half_copy.start()
    for copy in wo_copies():
        copy.start()

    lane = lax.broadcasted_iota(jnp.int32, (PATCHES, 128), 1)
    for image in range(2):
        rows = pl.ds(image * PATCHES, PATCHES)
        xf = x_ref[rows, :].astype(F32)
        both = jnp.where(
            lane == 0,
            jnp.sum(xf, axis=-1, keepdims=True),
            jnp.sum(xf * xf, axis=-1, keepdims=True),
        )
        stats[:, rows] = jnp.transpose(both)[0:8, :]

    pl.semaphore_wait(barrier, len(partners))

    mirror = {OPP: OPP, RIGHT: LEFT, LEFT: RIGHT}
    stat_copies = [
        remote(
            stats, stats_in.at[mirror[role]], stat_send.at[role], stat_recv.at[mirror[role]],
            line[role],
        )
        for role in (OPP, RIGHT, LEFT)
    ]
    for copy in stat_copies:
        copy.start()

    row = lax.broadcasted_iota(jnp.int32, (8, 2 * PATCHES), 1)
    places = jnp.full((8, 2 * PATCHES), RANKS * CAP, jnp.int32)
    for image in range(2):
        begin = image * PATCHES
        for piece in range(8):
            stop = begin + counts_ref[image, piece]
            places = jnp.where(
                (row >= begin) & (row < stop), dest_ref[image, piece] * CAP + row - begin, places
            )
            begin = stop
    target[gy] = places

    for copy in stat_copies:
        copy.wait()
    total = stats[...] + stats_in[0] + stats_in[1] + stats_in[2]

    def norm_copy(image):
        held = normed.at[gy * 2 + image]
        return remote(held, held, norm_send.at[image], norm_recv.at[image], sibling)

    for image in range(2):
        rows = pl.ds(image * PATCHES, PATCHES)
        part = total[:, image * PATCHES:(image + 1) * PATCHES]
        column = jnp.transpose(jnp.concatenate([part] * 16, axis=0))
        mean_value = column[:, 0:1] * (1.0 / D)
        spread = column[:, 1:2] * (1.0 / D) - mean_value * mean_value
        scale = lax.rsqrt(spread + EPS)
        xf = x_ref[rows, :].astype(F32)
        normed[gy * 2 + image] = ((xf - mean_value) * scale * gain_ref[...].reshape(1, BLOCK)).astype(BF16)
        norm_copy(image).start()

    target_copy = remote(target.at[gy], target.at[gy], target_send, target_recv, sibling)
    target_copy.start()
    cross_copy = remote(
        x_hbm.at[:, pl.ds(pl.multiple_of((1 - gy) * WIDE, WIDE), WIDE)],
        x_half.at[gy], half_send, half_recv, sibling,
    )
    cross_copy.start()

    def sum_copy(unit, kind):
        src, dst, role = {
            TWO_RIGHT: (two.at[unit, LOW], from_two_left.at[unit], RIGHT),
            TWO_LEFT: (two.at[unit, HIGH], from_two_right.at[unit], LEFT),
            RIGHT_HIGH: (to_right.at[unit, HIGH], from_left.at[unit, HIGH], RIGHT),
            LEFT_LOW: (to_left.at[unit, LOW], from_right.at[unit, LOW], LEFT),
            RIGHT_LOW: (to_right.at[unit, LOW], from_left.at[unit, LOW], RIGHT),
            LEFT_HIGH: (to_left.at[unit, HIGH], from_right.at[unit, HIGH], LEFT),
        }[kind]
        return remote(src, dst, sum_send.at[unit, kind], sum_recv.at[unit, kind], line[role])

    def att_copy(unit, kind):
        every = pl.ds(0, PATCHES)
        rows, source, place, role = {
            ATT_RIGHT: (every, OWN, LEFT, RIGHT),
            ATT_LEFT: (every, OWN, RIGHT, LEFT),
            PASS_RIGHT: (LOW, LEFT, OPP, RIGHT),
            PASS_LEFT: (HIGH, RIGHT, OPP, LEFT),
        }[kind]
        return remote(
            attended.at[unit, rows, pl.ds(source * 128, 128)],
            attended.at[unit, rows, pl.ds(place * 128, 128)],
            att_send.at[unit, kind], att_recv.at[unit, kind], line[role],
        )

    def part_copy(image):
        return remote(
            leaving.at[image], other.at[image], part_send.at[image], part_recv.at[image], sibling
        )

    def first_copy(group, step):
        return remote(
            outgoing.at[group, step - 1], middle.at[group, :, first_at],
            first_send.at[group, step - 1], first_recv.at[group, step - 1],
            (gx, gy, plane(lax.rem(first_at + step, RING), last_at)),
        )

    columns = {core: pl.ds(core * WIDE, WIDE) for core in range(2)}

    def last_copy(group, step, core):
        to = lax.rem(last_at + step, RING)
        if core == 0:
            dst = out_hbm.at[last_at, :, :, columns[core]]
        else:
            dst = out_hbm.at[:, last_at, :, columns[core]]
        return remote(
            middle.at[group, to], dst, last_send.at[group, step], last_recv.at[core, step],
            (gx, group, plane(first_at, to)),
        )

    def stay_copy(group, core):
        if core == 0:
            dst = out_hbm.at[last_at, :, :, columns[core]]
        else:
            dst = out_hbm.at[:, last_at, :, columns[core]]
        return pltpu.make_async_copy(middle.at[group, last_at], dst, local_sem)

    def product(unit, role):
        return jnp.dot(
            normed[lax.div(unit, SLOTS)], wq[role, lax.rem(unit, SLOTS)],
            preferred_element_type=F32,
        )

    def wait_weights(role, unit):
        for copy in wq_copies(role, lax.rem(unit, SLOTS)):
            copy.wait()

    def attend(unit):
        own = product(unit, OWN)
        for kind in (RIGHT_HIGH, LEFT_LOW, RIGHT_LOW, LEFT_HIGH):
            sum_copy(unit, kind).wait_recv()
        qkv = own + (from_left[unit].astype(F32) + from_right[unit].astype(F32))
        query = head_norm(qkv[:, 0:128], q_gain_ref[...])
        keys = head_norm(qkv[:, 128:256], k_gain_ref[...])
        values = qkv[:, 256:384].astype(BF16)
        scores = lax.dot_general(
            query, keys, (((1,), (1,)), ((), ())), preferred_element_type=F32
        ) * (1.0 / math.sqrt(128))
        expo = jnp.exp(scores)
        weights = (expo * (1.0 / jnp.sum(expo, axis=-1, keepdims=True))).astype(BF16)
        attended[unit, :, pl.ds(OWN * 128, 128)] = jnp.dot(
            weights, values, preferred_element_type=F32
        ).astype(BF16)
        att_copy(unit, ATT_RIGHT).start()
        att_copy(unit, ATT_LEFT).start()

    def project(image, side):
        parts = [
            jnp.dot(attended[image * SLOTS + slot], wo[side, slot], preferred_element_type=F32)
            for slot in range(SLOTS)
        ]
        return (parts[0] + parts[1] + parts[2]).astype(BF16)

    def route(group):
        for image in range(2):
            held = group * 2 + image
            part_copy(held).wait_recv()
            rows = pl.ds(image * PATCHES, PATCHES)
            layer[rows, :] = (
                x_half[group, rows, :].astype(F32)
                + (mine[held].astype(F32) + other[held].astype(F32))
            ).astype(BF16)
        place = lax.broadcasted_iota(jnp.int32, (RING * CAP, 1), 0)
        places = target[group][0:1, :]
        for step in (2, 1, 3, 0):
            rank = plane(lax.rem(first_at + step, RING), place >> 6)
            pick = jnp.where(rank * CAP + (place & (CAP - 1)) == places, 1.0, 0.0).astype(BF16)
            picked = jnp.dot(pick, layer[...], preferred_element_type=F32).astype(BF16)
            picked = picked.reshape(RING, CAP, WIDE)
            if step == 0:
                for to in range(RING):
                    middle[group, to, first_at] = picked[to]
            else:
                outgoing[group, step - 1] = picked
                first_copy(group, step).start()

    def route_on(group):
        for step in range(1, RING):
            first_copy(group, step).wait_recv()
        for core in range(2):
            @pl.when(gy == core)
            def _():
                for step in (2, 1, 3):
                    last_copy(group, step, core).start()

                @pl.when(group == gy)
                def _():
                    stay_copy(group, core).start()

                @pl.when(group != gy)
                def _():
                    last_copy(group, 0, core).start()

    def turn(step, carry):
        def back(count):
            return lax.rem(step + UNITS - count, UNITS)

        @pl.when((step >= 1) & (step <= UNITS))
        def _():
            unit = back(1)

            @pl.when(step <= SLOTS)
            def _():
                wait_weights(RIGHT, unit)
                wait_weights(LEFT, unit)

            to_right[unit] = product(unit, RIGHT).astype(BF16)
            sum_copy(unit, RIGHT_HIGH).start()
            to_left[unit] = product(unit, LEFT).astype(BF16)
            sum_copy(unit, LEFT_LOW).start()

        @pl.when(step < UNITS)
        def _():
            unit = back(0)
            image = lax.div(unit, SLOTS)

            @pl.when((lax.rem(unit, SLOTS) == 0) & (lax.div(image, 2) != gy))
            def _():
                norm_copy(lax.rem(image, 2)).wait_recv()

            @pl.when(step < SLOTS)
            def _():
                wait_weights(OPP, unit)

            two[unit] = product(unit, OPP).astype(BF16)
            sum_copy(unit, TWO_RIGHT).start()
            sum_copy(unit, TWO_LEFT).start()

        @pl.when((step >= 1) & (step <= UNITS))
        def _():
            unit = back(1)
            sum_copy(unit, TWO_RIGHT).wait_recv()
            to_right[unit, LOW, :] = (
                to_right[unit, LOW, :].astype(F32) + from_two_left[unit].astype(F32)
            ).astype(BF16)
            sum_copy(unit, RIGHT_LOW).start()
            sum_copy(unit, TWO_LEFT).wait_recv()
            to_left[unit, HIGH, :] = (
                to_left[unit, HIGH, :].astype(F32) + from_two_right[unit].astype(F32)
            ).astype(BF16)
            sum_copy(unit, LEFT_HIGH).start()

        @pl.when((step >= 2) & (step <= UNITS + 1))
        def _():
            unit = back(2)

            @pl.when(step < SLOTS + 2)
            def _():
                wait_weights(OWN, unit)

            attend(unit)

        @pl.when((step >= 3) & (step <= UNITS + 2))
        def _():
            unit = back(3)
            att_copy(unit, ATT_RIGHT).wait_recv()
            att_copy(unit, PASS_RIGHT).start()
            att_copy(unit, ATT_LEFT).wait_recv()
            att_copy(unit, PASS_LEFT).start()

        @pl.when((step >= 6) & (lax.rem(step, SLOTS) == 0))
        def _():
            image = lax.rem(lax.div(step, SLOTS) + 2, IMAGES)

            @pl.when(step == 6)
            def _():
                for copy in wo_copies():
                    copy.wait()
                half_copy.wait()
                target_copy.wait()
                cross_copy.wait()

            for slot in range(SLOTS):
                att_copy(image * SLOTS + slot, PASS_RIGHT).wait_recv()
                att_copy(image * SLOTS + slot, PASS_LEFT).wait_recv()
            leaving[image] = project(image, 0)
            part_copy(image).start()
            mine[image] = project(image, 1)

        @pl.when((step == 10) | (step == 15))
        def _():
            route(lax.div(step, 15))

        @pl.when((step == 12) | (step == 16))
        def _():
            route_on(lax.div(step, 16))

        return carry

    lax.fori_loop(0, UNITS + 5, turn, 0)

    def drain(unit, carry):
        for kind in range(6):
            sum_copy(unit, kind).wait_send()
        for kind in range(4):
            att_copy(unit, kind).wait_send()
        return carry

    lax.fori_loop(0, UNITS, drain, 0)
    for image in range(2):
        norm_copy(image).wait_send()
    for image in range(IMAGES):
        part_copy(image).wait_send()
    for group in range(2):
        for step in range(1, RING):
            first_copy(group, step).wait_send()
            last_copy(group, step, group).wait_send()
            last_copy(group, step, group).wait_recv()

        @pl.when(group != gy)
        def _():
            last_copy(group, 0, 0).wait_send()

    for core in range(2):
        @pl.when(core != gy)
        def _():
            last_copy(core, 0, core).wait_recv()

        @pl.when(core == gy)
        def _():
            stay_copy(core, core).wait()


def on_device(x_in, ln_gain, w_qkv, q_gain, k_gain, w_out, counts, dest):
    any_spec = pl.BlockSpec(memory_space=pl.ANY)
    vmem_spec = pl.BlockSpec(memory_space=pltpu.VMEM)
    smem_spec = pl.BlockSpec(memory_space=pltpu.SMEM)
    dma = pltpu.SemaphoreType.DMA
    routed = pl.pallas_call(
        kernel,
        out_shape=pltpu.VMEM((RING, RING, CAP, BLOCK), BF16),
        in_specs=[
            any_spec, vmem_spec, any_spec, vmem_spec, vmem_spec, any_spec, smem_spec, smem_spec,
        ],
        out_specs=any_spec,
        scratch_shapes=[
            pltpu.VMEM((2 * PATCHES, BLOCK), BF16),
            pltpu.VMEM((2, 2 * PATCHES, WIDE), BF16),
            pltpu.VMEM((IMAGES, PATCHES, BLOCK), BF16),
            pltpu.VMEM((4, SLOTS, BLOCK, GROUP), BF16),
            pltpu.VMEM((2, SLOTS, 4 * 128, WIDE), BF16),
            pltpu.VMEM((UNITS, PATCHES, GROUP), BF16),
            pltpu.VMEM((UNITS, PATCHES, GROUP), BF16),
            pltpu.VMEM((UNITS, PATCHES, GROUP), BF16),
            pltpu.VMEM((UNITS, HALF, GROUP), BF16),
            pltpu.VMEM((UNITS, HALF, GROUP), BF16),
            pltpu.VMEM((UNITS, PATCHES, GROUP), BF16),
            pltpu.VMEM((UNITS, PATCHES, GROUP), BF16),
            pltpu.VMEM((UNITS, PATCHES, 4 * 128), BF16),
            pltpu.VMEM((IMAGES, PATCHES, WIDE), BF16),
            pltpu.VMEM((IMAGES, PATCHES, WIDE), BF16),
            pltpu.VMEM((IMAGES, PATCHES, WIDE), BF16),
            pltpu.VMEM((2 * PATCHES, WIDE), BF16),
            pltpu.VMEM((2, RING - 1, RING, CAP, WIDE), BF16),
            pltpu.VMEM((2, RING, RING, CAP, WIDE), BF16),
            pltpu.VMEM((2, 8, 2 * PATCHES), jnp.int32),
            pltpu.VMEM((8, 2 * PATCHES), F32),
            pltpu.VMEM((3, 8, 2 * PATCHES), F32),
            dma(()),
            dma(()),
            dma((4, SLOTS, 3)),
            dma((2, SLOTS, 4)),
            dma(()),
            dma(()),
            dma(()),
            dma(()),
            dma((3,)),
            dma((3,)),
            dma((2,)),
            dma((2,)),
            dma((UNITS, 6)),
            dma((UNITS, 6)),
            dma((UNITS, 4)),
            dma((UNITS, 4)),
            dma((IMAGES,)),
            dma((IMAGES,)),
            dma((2, RING - 1)),
            dma((2, RING - 1)),
            dma((2, RING)),
            dma((2, RING)),
            dma(()),
        ],
        compiler_params=pltpu.CompilerParams(
            collective_id=0, has_side_effects=True, vmem_limit_bytes=58 * 2**20
        ),
        cost_estimate=pl.CostEstimate(
            flops=20 * 10**9, bytes_accessed=25 * 10**6, transcendentals=10**6
        ),
        name="layer",
    )(
        x_in.reshape(2 * PATCHES, BLOCK),
        ln_gain,
        jnp.transpose(w_qkv, (1, 2, 0, 3)),
        q_gain.reshape(1, 128),
        k_gain.reshape(1, 128),
        w_out.reshape(BLOCK, BLOCK),
        counts,
        dest,
    )
    return routed.reshape(1, 1, RANKS, 1, CAP, BLOCK)


def solution(mesh):
    in_specs = (
        P(("gy", "gz"), None, "gx"),
        P("gx"),
        P("gx", "gy", None, None),
        P(),
        P(),
        P("gy", None, "gx"),
        P(("gy", "gz"), None),
        P(("gy", "gz"), None),
    )
    out_specs = P("gy", "gz", None, None, None, "gx")
    return jax.shard_map(
        on_device, mesh=mesh, in_specs=in_specs, out_specs=out_specs, check_vma=False
    )
```

```python
import functools
import math

import jax
import jax.numpy as jnp
from jax import lax
from jax.experimental import pallas as pl
from jax.experimental.pallas import tpu as pltpu
from jax.sharding import PartitionSpec as P

D = 6144
PATCHES = 256
HALF = PATCHES // 2
BLOCK = 1536
WIDE = BLOCK // 2
GROUP = 384
SLOTS = 3
RANKS = 16
RING = 4
CAP = 64
IMAGES = 4
UNITS = IMAGES * SLOTS
EPS = 1e-06
MESH = pl.DeviceIdType.MESH
BF16 = jnp.bfloat16
F32 = jnp.float32

OPP, RIGHT, LEFT, OWN = 0, 1, 2, 3
TWO_RIGHT, TWO_LEFT, RIGHT_HIGH, LEFT_LOW, RIGHT_LOW, LEFT_HIGH = range(6)
ATT_RIGHT, ATT_LEFT, PASS_RIGHT, PASS_LEFT = range(4)
LOW = pl.ds(0, HALF)
HIGH = pl.ds(HALF, HALF)


def head_norm(values, gain):
    mean_value = jnp.mean(values, axis=-1, keepdims=True)
    spread = jnp.mean(values * values, axis=-1, keepdims=True) - mean_value * mean_value
    return ((values - mean_value) * lax.rsqrt(spread + EPS) * gain).astype(BF16)


def remote(src, dst, send_sem, recv_sem, device):
    return pltpu.make_async_remote_copy(
        src_ref=src,
        dst_ref=dst,
        send_sem=send_sem,
        recv_sem=recv_sem,
        device_id=device,
        device_id_type=MESH,
    )


def kernel(
    x_hbm, gain_hbm, wq_hbm, q_gain_hbm, k_gain_hbm, wo_hbm, counts_hbm, dest_hbm,
    out_hbm,
    x_ref, gain_ref, q_gain_ref, k_gain_ref, counts_ref, dest_ref, x_half, normed, wq, wo, two, to_right, to_left, from_two_left, from_two_right,
    from_left, from_right, attended, held, lead, fix, lead_out, lead_in, mine, leaving, other, layer, picks, outgoing, middle, target,
    stats, stats_in,
    x_sem, small_sem, half_sem, wq_sem, wo_sem, half_send, half_recv, target_send, target_recv,
    stat_send, stat_recv, lead_send, lead_recv, norm_send, norm_recv, sum_send, sum_recv, att_send, att_recv,
    part_send, part_recv, first_send, first_recv, last_send, last_recv, local_sem,
):
    gx, gy, gz = lax.axis_index("gx"), lax.axis_index("gy"), lax.axis_index("gz")
    at = {
        OPP: lax.rem(gx + 2, RING),
        RIGHT: lax.rem(gx + 1, RING),
        LEFT: lax.rem(gx + 3, RING),
        OWN: gx,
    }
    line = {role: (at[role], gy, gz) for role in (OPP, RIGHT, LEFT)}
    sibling = (gx, 1 - gy, gz)
    z_at, y_at = lax.div(gz, RING), lax.rem(gz, RING)
    first_at = (1 - gy) * y_at + gy * z_at
    last_at = (1 - gy) * z_at + gy * y_at

    def plane(first, last):
        return first * (1 + 3 * gy) + last * (4 - 3 * gy)

    def on_first(step):
        return plane(lax.rem(first_at + step, RING), last_at)

    def on_last(step):
        return plane(first_at, lax.rem(last_at + step, RING))

    barrier = pltpu.get_barrier_semaphore()
    partners = [line[OPP], line[RIGHT], line[LEFT], sibling]
    for step in range(1, RING):
        partners.append((gx, gy, on_first(step)))
        partners.append((gx, gy, on_last(step)))
        partners.append((gx, 1 - gy, on_first(step)))
    for partner in partners:
        pl.semaphore_signal(barrier, inc=1, device_id=partner, device_id_type=MESH)

    rows_of = [pl.ds(image * PATCHES, PATCHES) for image in range(2)]
    x_copies = [
        pltpu.make_async_copy(x_hbm.at[rows], x_ref.at[rows], x_sem.at[image])
        for image, rows in enumerate(rows_of)
    ]
    x_copies[0].start()
    small_copies = [
        pltpu.make_async_copy(src, dst, small_sem.at[k])
        for k, (src, dst) in enumerate((
            (gain_hbm, gain_ref), (q_gain_hbm, q_gain_ref), (k_gain_hbm, k_gain_ref),
            (counts_hbm, counts_ref), (dest_hbm, dest_ref),
        ))
    ]
    for copy in small_copies:
        copy.start()
    x_copies[1].start()

    def wq_copies(role, slot):
        return [
            pltpu.make_async_copy(
                wq_hbm.at[at[role] * SLOTS + slot, k],
                wq.at[role, slot, :, pl.ds(k * 128, 128)],
                wq_sem.at[role, slot, k],
            )
            for k in range(3)
        ]

    def wo_copies():
        for side in range(2):
            core = gy if side == 1 else 1 - gy
            for slot in range(SLOTS):
                for role in (OPP, RIGHT, LEFT, OWN):
                    row = pl.multiple_of((at[role] * SLOTS + slot) * 128, 128)
                    yield pltpu.make_async_copy(
                        wo_hbm.at[pl.ds(row, 128), pl.ds(pl.multiple_of(core * WIDE, WIDE), WIDE)],
                        wo.at[side, slot, pl.ds(role * 128, 128)],
                        wo_sem.at[side, slot, role],
                    )

    half_copy = pltpu.make_async_copy(
        x_hbm.at[:, pl.ds(pl.multiple_of(gy * WIDE, WIDE), WIDE)], x_half.at[gy], half_sem
    )

    def wait_weights(role, slot):
        for copy in wq_copies(role, slot):
            copy.wait()

    for role in (OPP, RIGHT, LEFT):
        for copy in wq_copies(role, 0):
            copy.start()
    def sum_copy(unit, kind):
        src, dst, role = {
            TWO_RIGHT: (two.at[unit, LOW], from_two_left.at[unit], RIGHT),
            TWO_LEFT: (two.at[unit, HIGH], from_two_right.at[unit], LEFT),
            RIGHT_HIGH: (to_right.at[unit, HIGH], from_left.at[unit, HIGH], RIGHT),
            LEFT_LOW: (to_left.at[unit, LOW], from_right.at[unit, LOW], LEFT),
            RIGHT_LOW: (to_right.at[unit, LOW], from_left.at[unit, LOW], RIGHT),
            LEFT_HIGH: (to_left.at[unit, HIGH], from_right.at[unit, HIGH], LEFT),
        }[kind]
        return remote(src, dst, sum_send.at[unit, kind], sum_recv.at[unit, kind], line[role])

    lane = lax.broadcasted_iota(jnp.int32, (PATCHES, 128), 1)
    mirror = {OPP: OPP, RIGHT: LEFT, LEFT: RIGHT}

    def stat_copies(image):
        return [
            remote(
                stats.at[image], stats_in.at[image, mirror[role]], stat_send.at[image, role],
                stat_recv.at[image, mirror[role]], line[role],
            )
            for role in (OPP, RIGHT, LEFT)
        ]

    def add_up(image):
        x_copies[image].wait()
        xf = x_ref[rows_of[image], :].astype(F32)
        sums = jnp.sum(xf, axis=-1, keepdims=True)
        both = jnp.where(lane == 0, sums, jnp.sum(xf * xf, axis=-1, keepdims=True))
        stats[image] = jnp.transpose(both)[0:8, :]
        return xf, sums

    for copy in small_copies:
        copy.wait()
    gain = gain_ref[...].reshape(1, BLOCK)
    xf, sums = add_up(0)
    lead[pl.ds(0, PATCHES), :] = ((xf - sums * (1.0 / BLOCK)) * gain).astype(BF16)
    high = gain.astype(BF16).astype(F32)
    line_at = lax.broadcasted_iota(jnp.int32, (16, BLOCK), 0)
    lead[pl.ds(PATCHES, 16), :] = jnp.where(
        line_at == 0, high, jnp.where(line_at == 1, gain - high, 0.0)
    ).astype(BF16)

    first_unit = 2 * SLOTS * gy

    def lead_product(role):
        full = jnp.dot(lead[...], wq[role, 0], preferred_element_type=F32)
        lead_out[role] = jnp.broadcast_to(
            full[PATCHES:PATCHES + 1, :] + full[PATCHES + 1:PATCHES + 2, :], (8, GROUP)
        )
        return full[0:PATCHES, :]

    lead_copies = [
        remote(
            lead_out.at[role], lead_in.at[mirror[role]], lead_send.at[role],
            lead_recv.at[mirror[role]], line[role],
        )
        for role in (OPP, RIGHT, LEFT)
    ]

    wait_weights(OPP, 0)
    two[first_unit] = lead_product(OPP).astype(BF16)
    for slot in range(SLOTS):
        for role in (OPP, RIGHT, LEFT, OWN):
            if slot != 0 or role == OWN:
                for copy in wq_copies(role, slot):
                    copy.start()

    pl.semaphore_wait(barrier, len(partners))

    for copy in stat_copies(0):
        copy.start()
    sum_copy(first_unit, TWO_RIGHT).start()
    sum_copy(first_unit, TWO_LEFT).start()
    wait_weights(RIGHT, 0)
    to_right[first_unit] = lead_product(RIGHT).astype(BF16)
    sum_copy(first_unit, RIGHT_HIGH).start()
    wait_weights(LEFT, 0)
    to_left[first_unit] = lead_product(LEFT).astype(BF16)
    sum_copy(first_unit, LEFT_LOW).start()
    add_up(1)
    for copy in stat_copies(1):
        copy.start()
    for copy in lead_copies:
        copy.start()

    def norm_copy(image):
        moved = normed.at[gy * 2 + image]
        return remote(moved, moved, norm_send.at[image], norm_recv.at[image], sibling)

    def normalize(image):
        for copy in stat_copies(image):
            copy.wait()
        shares = [stats_in[image, OPP], stats_in[image, RIGHT], stats_in[image, LEFT], stats[image]]
        total = shares[0] + shares[1] + shares[2] + shares[3]
        line_at = lax.broadcasted_iota(jnp.int32, (8, PATCHES), 0)
        part = jnp.where(line_at == 5, total[1:2, :], 0.0)
        for k, share in enumerate(shares + [total]):
            part = jnp.where(line_at == k, share[0:1, :], part)
        column = jnp.transpose(jnp.concatenate([part] * 16, axis=0))
        mean_value = column[:, 4:5] * (1.0 / D)
        spread = column[:, 5:6] * (1.0 / D) - mean_value * mean_value
        scale = lax.rsqrt(spread + EPS)
        if image == 0:
            fix[...] = jnp.where(lane == 4, scale, column * (1.0 / BLOCK) - mean_value)
        xf = x_ref[rows_of[image], :].astype(F32)
        normed[gy * 2 + image] = (
            (xf - mean_value) * scale * gain_ref[...].reshape(1, BLOCK)
        ).astype(BF16)
        norm_copy(image).start()

    def att_copy(unit, kind):
        every = pl.ds(0, PATCHES)
        rows, source, place, role = {
            ATT_RIGHT: (every, OWN, LEFT, RIGHT),
            ATT_LEFT: (every, OWN, RIGHT, LEFT),
            PASS_RIGHT: (LOW, LEFT, OPP, RIGHT),
            PASS_LEFT: (HIGH, RIGHT, OPP, LEFT),
        }[kind]
        return remote(
            attended.at[unit, rows, pl.ds(source * 128, 128)],
            attended.at[unit, rows, pl.ds(place * 128, 128)],
            att_send.at[unit, kind], att_recv.at[unit, kind], line[role],
        )

    def part_copy(image):
        return remote(
            leaving.at[image], other.at[image], part_send.at[image], part_recv.at[image], sibling
        )

    def first_copy(group, step):
        return remote(
            outgoing.at[group, step - 1], middle.at[group, :, first_at],
            first_send.at[group, step - 1], first_recv.at[group, step - 1],
            (gx, gy, on_first(step)),
        )

    columns = {core: pl.ds(core * WIDE, WIDE) for core in range(2)}

    def landing(core, source):
        if core == 0:
            return out_hbm.at[last_at, source, :, columns[core]]
        return out_hbm.at[source, last_at, :, columns[core]]

    def last_copy(group, hop, step, core):
        source = lax.rem(first_at + RING - hop, RING)
        return remote(
            middle.at[group, lax.rem(last_at + step, RING), source], landing(core, source),
            last_send.at[group, hop, step], last_recv.at[core, hop, step],
            (gx, group, on_last(step)),
        )

    def stay_copy(group, hop, core):
        source = lax.rem(first_at + RING - hop, RING)
        return pltpu.make_async_copy(
            middle.at[group, last_at, source], landing(core, source), local_sem.at[hop]
        )

    def product(unit, role):
        return jnp.dot(
            normed[lax.div(unit, SLOTS)], wq[role, lax.rem(unit, SLOTS)],
            preferred_element_type=F32,
        )

    def mend(values):
        for role in (OPP, RIGHT, LEFT):
            values = values + fix[:, role:role + 1] * lead_in[role][0:1, :]
        return fix[:, 4:5] * (values + fix[:, OWN:OWN + 1] * lead_out[OWN][0:1, :])

    def attend(unit, is_first):
        @pl.when(is_first)
        def _():
            held[...] = lead_product(OWN)
            for copy in lead_copies:
                copy.wait_recv()

        @pl.when(jnp.logical_not(is_first))
        def _():
            held[...] = product(unit, OWN)

        for kind in (RIGHT_HIGH, LEFT_LOW, RIGHT_LOW, LEFT_HIGH):
            sum_copy(unit, kind).wait_recv()
        held[...] += from_left[unit].astype(F32) + from_right[unit].astype(F32)

        @pl.when(is_first)
        def _():
            held[...] = mend(held[...])

        qkv = held[...]
        query = head_norm(qkv[:, 0:128], q_gain_ref[...])
        keys = head_norm(qkv[:, 128:256], k_gain_ref[...])
        values = qkv[:, 256:384].astype(BF16)
        scores = lax.dot_general(
            query, keys, (((1,), (1,)), ((), ())), preferred_element_type=F32
        ) * (1.0 / math.sqrt(128))
        expo = jnp.exp(scores)
        weights = (expo * (1.0 / jnp.sum(expo, axis=-1, keepdims=True))).astype(BF16)
        attended[unit, :, pl.ds(OWN * 128, 128)] = jnp.dot(
            weights, values, preferred_element_type=F32
        ).astype(BF16)
        att_copy(unit, ATT_RIGHT).start()
        att_copy(unit, ATT_LEFT).start()

    def project(image, side, slots):
        parts = [
            jnp.dot(attended[image * SLOTS + slot], wo[side, slot], preferred_element_type=F32)
            for slot in slots
        ]
        return parts[0] if len(parts) == 1 else parts[0] + parts[1]

    def route_on(group, hop):
        if hop != 0:
            first_copy(group, hop).wait_recv()
        for core in range(2):
            @pl.when(gy == core)
            def _():
                for step in (2, 1, 3):
                    last_copy(group, hop, step, core).start()

                @pl.when(group == gy)
                def _():
                    stay_copy(group, hop, core).start()

                @pl.when(group != gy)
                def _():
                    last_copy(group, hop, 0, core).start()

    def finish(held_image):
        part_copy(held_image).wait_recv()
        rows = pl.ds(pl.multiple_of(lax.rem(held_image, 2) * PATCHES, PATCHES), PATCHES)
        layer[rows, :] = (
            x_half[lax.div(held_image, 2), rows, :].astype(F32)
            + (mine[held_image].astype(F32) + other[held_image].astype(F32))
        ).astype(BF16)

    def prepare(group):
        finish(2 * group)
        place = lax.broadcasted_iota(jnp.int32, (RING * CAP, 1), 0)
        places = target[group][0:1, :]
        for step in range(RING):
            rank = plane(lax.rem(first_at + step, RING), place >> 6)
            picks[step] = jnp.where(
                rank * CAP + (place & (CAP - 1)) == places, 1.0, 0.0
            ).astype(BF16)

    def route(group):
        finish(2 * group + 1)
        for step in (2, 1, 3, 0):
            picked = jnp.dot(picks[step], layer[...], preferred_element_type=F32).astype(BF16)
            picked = picked.reshape(RING, CAP, WIDE)
            if step == 0:
                for to in range(RING):
                    middle[group, to, first_at] = picked[to]
                route_on(group, 0)
            else:
                outgoing[group, step - 1] = picked
                first_copy(group, step).start()

    def towards_opposite(unit):
        two[unit] = product(unit, OPP).astype(BF16)
        sum_copy(unit, TWO_RIGHT).start()
        sum_copy(unit, TWO_LEFT).start()

    normalize(0)
    sum_copy(first_unit, TWO_RIGHT).wait_recv()
    to_right[first_unit, LOW, :] = (
        to_right[first_unit, LOW, :].astype(F32) + from_two_left[first_unit].astype(F32)
    ).astype(BF16)
    sum_copy(first_unit, RIGHT_LOW).start()
    sum_copy(first_unit, TWO_LEFT).wait_recv()
    to_left[first_unit, HIGH, :] = (
        to_left[first_unit, HIGH, :].astype(F32) + from_two_right[first_unit].astype(F32)
    ).astype(BF16)
    sum_copy(first_unit, LEFT_HIGH).start()
    wait_weights(OPP, 1)

    @pl.when(gy == 0)
    def _():
        towards_opposite(1)

    normalize(1)

    @pl.when(gy == 1)
    def _():
        norm_copy(0).wait_recv()
        towards_opposite(0)

    row = lax.broadcasted_iota(jnp.int32, (8, 2 * PATCHES), 1)
    places = jnp.full((8, 2 * PATCHES), RANKS * CAP, jnp.int32)
    for image in range(2):
        begin = image * PATCHES
        for piece in range(8):
            stop = begin + counts_ref[image, piece]
            places = jnp.where(
                (row >= begin) & (row < stop), dest_ref[image, piece] * CAP + row - begin, places
            )
            begin = stop
    target[gy] = places
    target_copy = remote(target.at[gy], target.at[gy], target_send, target_recv, sibling)
    target_copy.start()
    cross_copy = remote(
        x_hbm.at[:, pl.ds(pl.multiple_of((1 - gy) * WIDE, WIDE), WIDE)],
        x_half.at[gy], half_send, half_recv, sibling,
    )
    cross_copy.start()
    half_copy.start()
    for copy in wo_copies():
        copy.start()

    def turn(step, carry):
        def back(count):
            at_turn = lax.rem(step + UNITS - count, UNITS)
            late = lax.div(at_turn, 2 * SLOTS + 1)
            shifted = lax.rem(at_turn + 2 * SLOTS, 2 * SLOTS + 1)
            return (1 - gy) * at_turn + gy * (late * at_turn + (1 - late) * shifted)

        @pl.when((step >= 2) & (step <= UNITS))
        def _():
            unit = back(1)

            @pl.when(step <= SLOTS)
            def _():
                wait_weights(RIGHT, lax.rem(step + 2, SLOTS))
                wait_weights(LEFT, lax.rem(step + 2, SLOTS))

            mine_right = product(unit, RIGHT)
            to_right[unit, HIGH, :] = mine_right[HALF:, :].astype(BF16)
            sum_copy(unit, RIGHT_HIGH).start()
            sum_copy(unit, TWO_RIGHT).wait_recv()
            to_right[unit, LOW, :] = (
                mine_right[:HALF, :] + from_two_left[unit].astype(F32)
            ).astype(BF16)
            sum_copy(unit, RIGHT_LOW).start()
            mine_left = product(unit, LEFT)
            to_left[unit, LOW, :] = mine_left[:HALF, :].astype(BF16)
            sum_copy(unit, LEFT_LOW).start()
            sum_copy(unit, TWO_LEFT).wait_recv()
            to_left[unit, HIGH, :] = (
                mine_left[HALF:, :] + from_two_right[unit].astype(F32)
            ).astype(BF16)
            sum_copy(unit, LEFT_HIGH).start()

        @pl.when((step >= 1) & (step <= UNITS - 2))
        def _():
            unit = back(-1)
            image = lax.div(unit, SLOTS)

            @pl.when((lax.rem(unit, SLOTS) == 0) & (lax.div(image, 2) != gy))
            def _():
                norm_copy(lax.rem(image, 2)).wait_recv()

            @pl.when(step == 1)
            def _():
                wait_weights(OPP, 2)

            towards_opposite(unit)

        @pl.when((step >= 2) & (step <= UNITS + 1))
        def _():
            unit = back(2)

            @pl.when(step < SLOTS + 2)
            def _():
                wait_weights(OWN, lax.rem(step + 1, SLOTS))

            attend(unit, step == 2)

        @pl.when((step >= 3) & (step <= UNITS + 2))
        def _():
            unit = back(3)
            att_copy(unit, ATT_RIGHT).wait_recv()
            att_copy(unit, PASS_RIGHT).start()
            att_copy(unit, ATT_LEFT).wait_recv()
            att_copy(unit, PASS_LEFT).start()

        @pl.when((step == 7) | (step == 10) | (step == 12) | (step == 16))
        def _():
            image = lax.div(step, 4) - 1

            @pl.when(step == 7)
            def _():
                for copy in wo_copies():
                    copy.wait()
                half_copy.wait()
                target_copy.wait()
                cross_copy.wait()

            def wait_slot(slot):
                att_copy(image * SLOTS + slot, PASS_RIGHT).wait_recv()
                att_copy(image * SLOTS + slot, PASS_LEFT).wait_recv()

            @pl.when(lax.rem(image, 2) == 1)
            def _():
                prepare(lax.div(image, 2))

            wait_slot(0)
            wait_slot(1)
            early = [project(image, side, (0, 1)) for side in range(2)]
            wait_slot(2)
            leaving[image] = (early[0] + project(image, 0, (2,))).astype(BF16)
            part_copy(image).start()
            mine[image] = (early[1] + project(image, 1, (2,))).astype(BF16)

        @pl.when((step == 10) | (step == 16))
        def _():
            route(lax.div(step, 16))

        @pl.when((step == 12) | (step == 17))
        def _():
            for hop in (1, 3, 2):
                route_on(lax.div(step, 17), hop)

        return carry

    lax.fori_loop(1, UNITS + 6, turn, 0)

    def drain(unit, carry):
        for kind in range(6):
            sum_copy(unit, kind).wait_send()
        for kind in range(4):
            att_copy(unit, kind).wait_send()
        return carry

    lax.fori_loop(0, UNITS, drain, 0)
    for copy in lead_copies:
        copy.wait_send()
    for image in range(2):
        norm_copy(image).wait_send()
    for image in range(IMAGES):
        part_copy(image).wait_send()
    for group in range(2):
        for step in range(1, RING):
            first_copy(group, step).wait_send()
        for hop in range(RING):
            for step in range(1, RING):
                last_copy(group, hop, step, group).wait_send()
                last_copy(group, hop, step, group).wait_recv()

            @pl.when(group != gy)
            def _():
                last_copy(group, hop, 0, group).wait_send()
                last_copy(group, hop, 0, group).wait_recv()

            @pl.when(group == gy)
            def _():
                stay_copy(group, hop, group).wait()


def on_device(x_in, ln_gain, w_qkv, q_gain, k_gain, w_out, counts, dest):
    any_spec = pl.BlockSpec(memory_space=pl.ANY)
    dma = pltpu.SemaphoreType.DMA
    routed = pl.pallas_call(
        kernel,
        out_shape=pltpu.VMEM((RING, RING, CAP, BLOCK), BF16),
        in_specs=[any_spec] * 8,
        out_specs=any_spec,
        scratch_shapes=[
            pltpu.VMEM((2 * PATCHES, BLOCK), BF16),
            pltpu.VMEM((BLOCK,), F32),
            pltpu.VMEM((1, 128), F32),
            pltpu.VMEM((1, 128), F32),
            pltpu.SMEM((2, 8), jnp.int32),
            pltpu.SMEM((2, 8), jnp.int32),
            pltpu.VMEM((2, 2 * PATCHES, WIDE), BF16),
            pltpu.VMEM((IMAGES, PATCHES, BLOCK), BF16),
            pltpu.VMEM((4, SLOTS, BLOCK, GROUP), BF16),
            pltpu.VMEM((2, SLOTS, 4 * 128, WIDE), BF16),
            pltpu.VMEM((UNITS, PATCHES, GROUP), BF16),
            pltpu.VMEM((UNITS, PATCHES, GROUP), BF16),
            pltpu.VMEM((UNITS, PATCHES, GROUP), BF16),
            pltpu.VMEM((UNITS, HALF, GROUP), BF16),
            pltpu.VMEM((UNITS, HALF, GROUP), BF16),
            pltpu.VMEM((UNITS, PATCHES, GROUP), BF16),
            pltpu.VMEM((UNITS, PATCHES, GROUP), BF16),
            pltpu.VMEM((UNITS, PATCHES, 4 * 128), BF16),
            pltpu.VMEM((PATCHES, GROUP), F32),
            pltpu.VMEM((PATCHES + 16, BLOCK), BF16),
            pltpu.VMEM((PATCHES, 128), F32),
            pltpu.VMEM((4, 8, GROUP), F32),
            pltpu.VMEM((3, 8, GROUP), F32),
            pltpu.VMEM((IMAGES, PATCHES, WIDE), BF16),
            pltpu.VMEM((IMAGES, PATCHES, WIDE), BF16),
            pltpu.VMEM((IMAGES, PATCHES, WIDE), BF16),
            pltpu.VMEM((2 * PATCHES, WIDE), BF16),
            pltpu.VMEM((RING, RING * CAP, 2 * PATCHES), BF16),
            pltpu.VMEM((2, RING - 1, RING, CAP, WIDE), BF16),
            pltpu.VMEM((2, RING, RING, CAP, WIDE), BF16),
            pltpu.VMEM((2, 8, 2 * PATCHES), jnp.int32),
            pltpu.VMEM((2, 8, PATCHES), F32),
            pltpu.VMEM((2, 3, 8, PATCHES), F32),
            dma((2,)),
            dma((5,)),
            dma(()),
            dma((4, SLOTS, 3)),
            dma((2, SLOTS, 4)),
            dma(()),
            dma(()),
            dma(()),
            dma(()),
            dma((2, 3)),
            dma((2, 3)),
            dma((3,)),
            dma((3,)),
            dma((2,)),
            dma((2,)),
            dma((UNITS, 6)),
            dma((UNITS, 6)),
            dma((UNITS, 4)),
            dma((UNITS, 4)),
            dma((IMAGES,)),
            dma((IMAGES,)),
            dma((2, RING - 1)),
            dma((2, RING - 1)),
            dma((2, RING, RING)),
            dma((2, RING, RING)),
            dma((RING,)),
        ],
        compiler_params=pltpu.CompilerParams(
            collective_id=0, has_side_effects=True, vmem_limit_bytes=58 * 2**20
        ),
        cost_estimate=pl.CostEstimate(
            flops=20 * 10**9, bytes_accessed=25 * 10**6, transcendentals=10**6
        ),
        name="layer",
    )(
        x_in.reshape(2 * PATCHES, BLOCK),
        ln_gain,
        jnp.transpose(w_qkv, (1, 2, 0, 3)),
        q_gain.reshape(1, 128),
        k_gain.reshape(1, 128),
        w_out.reshape(BLOCK, BLOCK),
        counts,
        dest,
    )
    return routed.reshape(1, 1, RANKS, 1, CAP, BLOCK)


def solution(mesh):
    in_specs = (
        P(("gy", "gz"), None, "gx"),
        P("gx"),
        P("gx", "gy", None, None),
        P(),
        P(),
        P("gy", None, "gx"),
        P(("gy", "gz"), None),
        P(("gy", "gz"), None),
    )
    out_specs = P("gy", "gz", None, None, None, "gx")
    return jax.shard_map(
        on_device, mesh=mesh, in_specs=in_specs, out_specs=out_specs, check_vma=False
    )
```

```python
import functools
import math

import jax
import jax.numpy as jnp
from jax import lax
from jax.experimental import pallas as pl
from jax.experimental.pallas import tpu as pltpu
from jax.sharding import PartitionSpec as P

D = 6144
PATCHES = 256
HALF = PATCHES // 2
BLOCK = 1536
WIDE = BLOCK // 2
GROUP = 384
SLOTS = 3
RANKS = 16
RING = 4
CAP = 64
IMAGES = 4
UNITS = IMAGES * SLOTS
EPS = 1e-06
MESH = pl.DeviceIdType.MESH
BF16 = jnp.bfloat16
F32 = jnp.float32

OPP, RIGHT, LEFT, OWN = 0, 1, 2, 3
TWO_RIGHT, TWO_LEFT, RIGHT_HIGH, LEFT_LOW, RIGHT_LOW, LEFT_HIGH = range(6)
ATT_RIGHT, ATT_LEFT, PASS_RIGHT, PASS_LEFT = range(4)
LOW = pl.ds(0, HALF)
HIGH = pl.ds(HALF, HALF)


def head_norm(values, gain):
    mean_value = jnp.mean(values, axis=-1, keepdims=True)
    spread = jnp.mean(values * values, axis=-1, keepdims=True) - mean_value * mean_value
    return ((values - mean_value) * lax.rsqrt(spread + EPS) * gain).astype(BF16)


def remote(src, dst, send_sem, recv_sem, device):
    return pltpu.make_async_remote_copy(
        src_ref=src,
        dst_ref=dst,
        send_sem=send_sem,
        recv_sem=recv_sem,
        device_id=device,
        device_id_type=MESH,
    )


def kernel(
    x_hbm, gain_hbm, wq_hbm, q_gain_hbm, k_gain_hbm, wo_hbm, counts_hbm, dest_hbm,
    out_hbm,
    x_ref, gain_ref, q_gain_ref, k_gain_ref, counts_ref, dest_ref, x_half, normed, wq, wo, two, to_right, to_left, from_two_left, from_two_right,
    from_left, from_right, attended, held, lead, fix, lead_out, lead_in, mine, leaving, other, layer, picks, outgoing, middle, target,
    stats, stats_in,
    x_sem, small_sem, half_sem, wq_sem, wo_sem, half_send, half_recv, target_send, target_recv,
    stat_send, stat_recv, lead_send, lead_recv, norm_send, norm_recv, sum_send, sum_recv, att_send, att_recv,
    part_send, part_recv, first_send, first_recv, last_send, last_recv, local_sem,
):
    gx, gy, gz = lax.axis_index("gx"), lax.axis_index("gy"), lax.axis_index("gz")
    at = {
        OPP: lax.rem(gx + 2, RING),
        RIGHT: lax.rem(gx + 1, RING),
        LEFT: lax.rem(gx + 3, RING),
        OWN: gx,
    }
    line = {role: (at[role], gy, gz) for role in (OPP, RIGHT, LEFT)}
    sibling = (gx, 1 - gy, gz)
    z_at, y_at = lax.div(gz, RING), lax.rem(gz, RING)
    first_at = (1 - gy) * y_at + gy * z_at
    last_at = (1 - gy) * z_at + gy * y_at

    def plane(first, last):
        return first * (1 + 3 * gy) + last * (4 - 3 * gy)

    def on_first(step):
        return plane(lax.rem(first_at + step, RING), last_at)

    def on_last(step):
        return plane(first_at, lax.rem(last_at + step, RING))

    barrier = pltpu.get_barrier_semaphore()
    partners = [line[OPP], line[RIGHT], line[LEFT], sibling]
    for step in range(1, RING):
        partners.append((gx, gy, on_first(step)))
        partners.append((gx, gy, on_last(step)))
        partners.append((gx, 1 - gy, on_first(step)))
    for partner in partners:
        pl.semaphore_signal(barrier, inc=1, device_id=partner, device_id_type=MESH)

    rows_of = [pl.ds(image * PATCHES, PATCHES) for image in range(2)]
    x_copies = [
        pltpu.make_async_copy(x_hbm.at[rows], x_ref.at[rows], x_sem.at[image])
        for image, rows in enumerate(rows_of)
    ]
    x_copies[0].start()
    small_copies = [
        pltpu.make_async_copy(src, dst, small_sem.at[k])
        for k, (src, dst) in enumerate((
            (gain_hbm, gain_ref), (q_gain_hbm, q_gain_ref), (k_gain_hbm, k_gain_ref),
            (counts_hbm, counts_ref), (dest_hbm, dest_ref),
        ))
    ]
    for copy in small_copies:
        copy.start()
    x_copies[1].start()

    def wq_copies(role, slot):
        return [
            pltpu.make_async_copy(
                wq_hbm.at[at[role] * SLOTS + slot, k],
                wq.at[role, slot, :, pl.ds(k * 128, 128)],
                wq_sem.at[role, slot, k],
            )
            for k in range(3)
        ]

    def wo_copies():
        for side in range(2):
            core = gy if side == 1 else 1 - gy
            for slot in range(SLOTS):
                for role in (OPP, RIGHT, LEFT, OWN):
                    row = pl.multiple_of((at[role] * SLOTS + slot) * 128, 128)
                    yield pltpu.make_async_copy(
                        wo_hbm.at[pl.ds(row, 128), pl.ds(pl.multiple_of(core * WIDE, WIDE), WIDE)],
                        wo.at[side, slot, pl.ds(role * 128, 128)],
                        wo_sem.at[side, slot, role],
                    )

    half_copy = pltpu.make_async_copy(
        x_hbm.at[:, pl.ds(pl.multiple_of(gy * WIDE, WIDE), WIDE)], x_half.at[gy], half_sem
    )

    def wait_weights(role, slot):
        for copy in wq_copies(role, slot):
            copy.wait()

    for role in (OPP, RIGHT, LEFT):
        for copy in wq_copies(role, 0):
            copy.start()
    def sum_copy(unit, kind):
        src, dst, role = {
            TWO_RIGHT: (two.at[unit, LOW], from_two_left.at[unit], RIGHT),
            TWO_LEFT: (two.at[unit, HIGH], from_two_right.at[unit], LEFT),
            RIGHT_HIGH: (to_right.at[unit, HIGH], from_left.at[unit, HIGH], RIGHT),
            LEFT_LOW: (to_left.at[unit, LOW], from_right.at[unit, LOW], LEFT),
            RIGHT_LOW: (to_right.at[unit, LOW], from_left.at[unit, LOW], RIGHT),
            LEFT_HIGH: (to_left.at[unit, HIGH], from_right.at[unit, HIGH], LEFT),
        }[kind]
        return remote(src, dst, sum_send.at[unit, kind], sum_recv.at[unit, kind], line[role])

    lane = lax.broadcasted_iota(jnp.int32, (PATCHES, 128), 1)
    mirror = {OPP: OPP, RIGHT: LEFT, LEFT: RIGHT}

    def stat_copies(image):
        return [
            remote(
                stats.at[image], stats_in.at[image, mirror[role]], stat_send.at[image, role],
                stat_recv.at[image, mirror[role]], line[role],
            )
            for role in (OPP, RIGHT, LEFT)
        ]

    def add_up(image):
        x_copies[image].wait()
        xf = x_ref[rows_of[image], :].astype(F32)
        sums = jnp.sum(xf, axis=-1, keepdims=True)
        both = jnp.where(lane == 0, sums, jnp.sum(xf * xf, axis=-1, keepdims=True))
        stats[image] = jnp.transpose(both)[0:8, :]
        return xf, sums

    for copy in small_copies:
        copy.wait()
    gain = gain_ref[...].reshape(1, BLOCK)
    xf, sums = add_up(0)
    lead[pl.ds(0, PATCHES), :] = ((xf - sums * (1.0 / BLOCK)) * gain).astype(BF16)
    high = gain.astype(BF16).astype(F32)
    line_at = lax.broadcasted_iota(jnp.int32, (16, BLOCK), 0)
    lead[pl.ds(PATCHES, 16), :] = jnp.where(
        line_at == 0, high, jnp.where(line_at == 1, gain - high, 0.0)
    ).astype(BF16)

    first_unit = 2 * SLOTS * gy

    def lead_product(role):
        full = jnp.dot(lead[...], wq[role, 0], preferred_element_type=F32)
        lead_out[role] = jnp.broadcast_to(
            full[PATCHES:PATCHES + 1, :] + full[PATCHES + 1:PATCHES + 2, :], (8, GROUP)
        )
        return full[0:PATCHES, :]

    lead_copies = [
        remote(
            lead_out.at[role], lead_in.at[mirror[role]], lead_send.at[role],
            lead_recv.at[mirror[role]], line[role],
        )
        for role in (OPP, RIGHT, LEFT)
    ]

    wait_weights(OPP, 0)
    two[first_unit] = lead_product(OPP).astype(BF16)
    for slot in range(SLOTS):
        for role in (OPP, RIGHT, LEFT, OWN):
            if slot != 0 or role == OWN:
                for copy in wq_copies(role, slot):
                    copy.start()

    pl.semaphore_wait(barrier, len(partners))

    for copy in stat_copies(0):
        copy.start()
    sum_copy(first_unit, TWO_RIGHT).start()
    sum_copy(first_unit, TWO_LEFT).start()
    wait_weights(RIGHT, 0)
    to_right[first_unit] = lead_product(RIGHT).astype(BF16)
    sum_copy(first_unit, RIGHT_HIGH).start()
    wait_weights(LEFT, 0)
    to_left[first_unit] = lead_product(LEFT).astype(BF16)
    sum_copy(first_unit, LEFT_LOW).start()
    add_up(1)
    for copy in stat_copies(1):
        copy.start()
    for copy in lead_copies:
        copy.start()

    def norm_copy(image):
        moved = normed.at[gy * 2 + image]
        return remote(moved, moved, norm_send.at[image], norm_recv.at[image], sibling)

    def normalize(image):
        for copy in stat_copies(image):
            copy.wait()
        shares = [stats_in[image, OPP], stats_in[image, RIGHT], stats_in[image, LEFT], stats[image]]
        total = shares[0] + shares[1] + shares[2] + shares[3]
        line_at = lax.broadcasted_iota(jnp.int32, (8, PATCHES), 0)
        part = jnp.where(line_at == 5, total[1:2, :], 0.0)
        for k, share in enumerate(shares + [total]):
            part = jnp.where(line_at == k, share[0:1, :], part)
        column = jnp.transpose(jnp.concatenate([part] * 16, axis=0))
        mean_value = column[:, 4:5] * (1.0 / D)
        spread = column[:, 5:6] * (1.0 / D) - mean_value * mean_value
        scale = lax.rsqrt(spread + EPS)
        if image == 0:
            fix[...] = jnp.where(lane == 4, scale, column * (1.0 / BLOCK) - mean_value)
        xf = x_ref[rows_of[image], :].astype(F32)
        normed[gy * 2 + image] = (
            (xf - mean_value) * scale * gain_ref[...].reshape(1, BLOCK)
        ).astype(BF16)
        norm_copy(image).start()

    def att_copy(unit, kind):
        every = pl.ds(0, PATCHES)
        rows, source, place, role = {
            ATT_RIGHT: (every, OWN, LEFT, RIGHT),
            ATT_LEFT: (every, OWN, RIGHT, LEFT),
            PASS_RIGHT: (LOW, LEFT, OPP, RIGHT),
            PASS_LEFT: (HIGH, RIGHT, OPP, LEFT),
        }[kind]
        return remote(
            attended.at[unit, rows, pl.ds(source * 128, 128)],
            attended.at[unit, rows, pl.ds(place * 128, 128)],
            att_send.at[unit, kind], att_recv.at[unit, kind], line[role],
        )

    def part_copy(image):
        return remote(
            leaving.at[image], other.at[image], part_send.at[image], part_recv.at[image], sibling
        )

    def first_copy(group, hop, step):
        to = lax.rem(last_at + step, RING)
        return remote(
            outgoing.at[group, hop - 1, to], middle.at[group, to, first_at],
            first_send.at[group, hop - 1, step], first_recv.at[group, hop - 1, step],
            (gx, gy, on_first(hop)),
        )

    columns = {core: pl.ds(core * WIDE, WIDE) for core in range(2)}

    def landing(core, source):
        if core == 0:
            return out_hbm.at[last_at, source, :, columns[core]]
        return out_hbm.at[source, last_at, :, columns[core]]

    def last_copy(group, hop, step, core):
        source = lax.rem(first_at + RING - hop, RING)
        return remote(
            middle.at[group, lax.rem(last_at + step, RING), source], landing(core, source),
            last_send.at[group, hop, step], last_recv.at[core, hop, step],
            (gx, group, on_last(step)),
        )

    def stay_copy(group, hop, core):
        source = lax.rem(first_at + RING - hop, RING)
        return pltpu.make_async_copy(
            middle.at[group, last_at, source], landing(core, source), local_sem.at[hop]
        )

    def product(unit, role):
        return jnp.dot(
            normed[lax.div(unit, SLOTS)], wq[role, lax.rem(unit, SLOTS)],
            preferred_element_type=F32,
        )

    def mend(values):
        for role in (OPP, RIGHT, LEFT):
            values = values + fix[:, role:role + 1] * lead_in[role][0:1, :]
        return fix[:, 4:5] * (values + fix[:, OWN:OWN + 1] * lead_out[OWN][0:1, :])

    def attend(unit, is_first):
        @pl.when(is_first)
        def _():
            held[...] = lead_product(OWN)
            for copy in lead_copies:
                copy.wait_recv()

        @pl.when(jnp.logical_not(is_first))
        def _():
            held[...] = product(unit, OWN)

        for kind in (RIGHT_HIGH, LEFT_LOW, RIGHT_LOW, LEFT_HIGH):
            sum_copy(unit, kind).wait_recv()
        held[...] += from_left[unit].astype(F32) + from_right[unit].astype(F32)

        @pl.when(is_first)
        def _():
            held[...] = mend(held[...])

        qkv = held[...]
        query = head_norm(qkv[:, 0:128], q_gain_ref[...])
        keys = head_norm(qkv[:, 128:256], k_gain_ref[...])
        values = qkv[:, 256:384].astype(BF16)
        scores = lax.dot_general(
            query, keys, (((1,), (1,)), ((), ())), preferred_element_type=F32
        ) * (1.0 / math.sqrt(128))
        expo = jnp.exp(scores)
        weights = (expo * (1.0 / jnp.sum(expo, axis=-1, keepdims=True))).astype(BF16)
        attended[unit, :, pl.ds(OWN * 128, 128)] = jnp.dot(
            weights, values, preferred_element_type=F32
        ).astype(BF16)
        att_copy(unit, ATT_RIGHT).start()
        att_copy(unit, ATT_LEFT).start()

    def project(image, side, slots):
        parts = [
            jnp.dot(attended[image * SLOTS + slot], wo[side, slot], preferred_element_type=F32)
            for slot in slots
        ]
        return parts[0] if len(parts) == 1 else parts[0] + parts[1]

    def send_last(group, hop, step):
        for core in range(2):
            @pl.when(gy == core)
            def _():
                if step != 0:
                    last_copy(group, hop, step, core).start()
                else:
                    @pl.when(group == gy)
                    def _():
                        stay_copy(group, hop, core).start()

                    @pl.when(group != gy)
                    def _():
                        last_copy(group, hop, 0, core).start()

    def route_on(group):
        for hop in (1, 3, 2):
            for step in (2, 1, 3):
                first_copy(group, hop, step).wait_recv()
                send_last(group, hop, step)
        for hop in range(1, RING):
            first_copy(group, hop, 0).wait_recv()
            send_last(group, hop, 0)

    def finish(held_image):
        part_copy(held_image).wait_recv()
        rows = pl.ds(pl.multiple_of(lax.rem(held_image, 2) * PATCHES, PATCHES), PATCHES)
        layer[rows, :] = (
            x_half[lax.div(held_image, 2), rows, :].astype(F32)
            + (mine[held_image].astype(F32) + other[held_image].astype(F32))
        ).astype(BF16)

    def prepare(group):
        finish(2 * group)
        place = lax.broadcasted_iota(jnp.int32, (RING * CAP, 1), 0)
        places = target[group][0:1, :]
        for step in range(RING):
            rank = plane(lax.rem(first_at + step, RING), place >> 6)
            picks[step] = jnp.where(
                rank * CAP + (place & (CAP - 1)) == places, 1.0, 0.0
            ).astype(BF16)

    def route(group):
        finish(2 * group + 1)
        for step in (1, 3, 2, 0):
            picked = jnp.dot(picks[step], layer[...], preferred_element_type=F32).astype(BF16)
            picked = picked.reshape(RING, CAP, WIDE)
            if step == 0:
                for to in range(RING):
                    middle[group, to, first_at] = picked[to]
            else:
                outgoing[group, step - 1] = picked
                for on in (2, 1, 3):
                    first_copy(group, step, on).start()
        for step in (1, 3, 2):
            first_copy(group, step, 0).start()
        for on in (2, 1, 3, 0):
            send_last(group, 0, on)

    def towards_opposite(unit):
        two[unit] = product(unit, OPP).astype(BF16)
        sum_copy(unit, TWO_RIGHT).start()
        sum_copy(unit, TWO_LEFT).start()

    normalize(0)
    sum_copy(first_unit, TWO_RIGHT).wait_recv()
    to_right[first_unit, LOW, :] = (
        to_right[first_unit, LOW, :].astype(F32) + from_two_left[first_unit].astype(F32)
    ).astype(BF16)
    sum_copy(first_unit, RIGHT_LOW).start()
    sum_copy(first_unit, TWO_LEFT).wait_recv()
    to_left[first_unit, HIGH, :] = (
        to_left[first_unit, HIGH, :].astype(F32) + from_two_right[first_unit].astype(F32)
    ).astype(BF16)
    sum_copy(first_unit, LEFT_HIGH).start()
    wait_weights(OPP, 1)

    @pl.when(gy == 0)
    def _():
        towards_opposite(1)

    normalize(1)

    @pl.when(gy == 1)
    def _():
        norm_copy(0).wait_recv()
        towards_opposite(0)

    row = lax.broadcasted_iota(jnp.int32, (8, 2 * PATCHES), 1)
    places = jnp.full((8, 2 * PATCHES), RANKS * CAP, jnp.int32)
    for image in range(2):
        begin = image * PATCHES
        for piece in range(8):
            stop = begin + counts_ref[image, piece]
            places = jnp.where(
                (row >= begin) & (row < stop), dest_ref[image, piece] * CAP + row - begin, places
            )
            begin = stop
    target[gy] = places
    target_copy = remote(target.at[gy], target.at[gy], target_send, target_recv, sibling)
    target_copy.start()
    cross_copy = remote(
        x_hbm.at[:, pl.ds(pl.multiple_of((1 - gy) * WIDE, WIDE), WIDE)],
        x_half.at[gy], half_send, half_recv, sibling,
    )
    cross_copy.start()
    half_copy.start()
    for copy in wo_copies():
        copy.start()

    def turn(step, carry):
        def back(count):
            at_turn = lax.rem(step + UNITS - count, UNITS)
            late = lax.div(at_turn, 2 * SLOTS + 1)
            shifted = lax.rem(at_turn + 2 * SLOTS, 2 * SLOTS + 1)
            return (1 - gy) * at_turn + gy * (late * at_turn + (1 - late) * shifted)

        @pl.when((step == 9) | (step == 14))
        def _():
            prepare(lax.div(step, 14))

        @pl.when((step >= 2) & (step <= UNITS))
        def _():
            unit = back(1)

            @pl.when(step <= SLOTS)
            def _():
                wait_weights(RIGHT, lax.rem(step + 2, SLOTS))
                wait_weights(LEFT, lax.rem(step + 2, SLOTS))

            mine_right = product(unit, RIGHT)
            to_right[unit, HIGH, :] = mine_right[HALF:, :].astype(BF16)
            sum_copy(unit, RIGHT_HIGH).start()
            sum_copy(unit, TWO_RIGHT).wait_recv()
            to_right[unit, LOW, :] = (
                mine_right[:HALF, :] + from_two_left[unit].astype(F32)
            ).astype(BF16)
            sum_copy(unit, RIGHT_LOW).start()
            mine_left = product(unit, LEFT)
            to_left[unit, LOW, :] = mine_left[:HALF, :].astype(BF16)
            sum_copy(unit, LEFT_LOW).start()
            sum_copy(unit, TWO_LEFT).wait_recv()
            to_left[unit, HIGH, :] = (
                mine_left[HALF:, :] + from_two_right[unit].astype(F32)
            ).astype(BF16)
            sum_copy(unit, LEFT_HIGH).start()

        @pl.when((step >= 1) & (step <= UNITS - 2))
        def _():
            unit = back(-1)
            image = lax.div(unit, SLOTS)

            @pl.when((lax.rem(unit, SLOTS) == 0) & (lax.div(image, 2) != gy))
            def _():
                norm_copy(lax.rem(image, 2)).wait_recv()

            @pl.when(step == 1)
            def _():
                wait_weights(OPP, 2)

            towards_opposite(unit)

        @pl.when((step >= 2) & (step <= UNITS + 1))
        def _():
            unit = back(2)

            @pl.when(step < SLOTS + 2)
            def _():
                wait_weights(OWN, lax.rem(step + 1, SLOTS))

            attend(unit, step == 2)

        @pl.when((step >= 3) & (step <= UNITS + 2))
        def _():
            unit = back(3)
            att_copy(unit, ATT_RIGHT).wait_recv()
            att_copy(unit, PASS_RIGHT).start()
            att_copy(unit, ATT_LEFT).wait_recv()
            att_copy(unit, PASS_LEFT).start()

        @pl.when((step == 7) | (step == 10) | (step == 12) | (step == 16))
        def _():
            image = lax.div(step, 4) - 1

            @pl.when(step == 7)
            def _():
                for copy in wo_copies():
                    copy.wait()
                half_copy.wait()
                target_copy.wait()
                cross_copy.wait()

            def wait_slot(slot):
                att_copy(image * SLOTS + slot, PASS_RIGHT).wait_recv()
                att_copy(image * SLOTS + slot, PASS_LEFT).wait_recv()

            wait_slot(0)
            wait_slot(1)
            early = [project(image, side, (0, 1)) for side in range(2)]
            wait_slot(2)
            leaving[image] = (early[0] + project(image, 0, (2,))).astype(BF16)
            part_copy(image).start()
            mine[image] = (early[1] + project(image, 1, (2,))).astype(BF16)

        @pl.when((step == 10) | (step == 16))
        def _():
            route(lax.div(step, 16))

        @pl.when((step == 12) | (step == 17))
        def _():
            route_on(lax.div(step, 17))

        return carry

    lax.fori_loop(1, UNITS + 6, turn, 0)

    def drain(unit, carry):
        for kind in range(6):
            sum_copy(unit, kind).wait_send()
        for kind in range(4):
            att_copy(unit, kind).wait_send()
        return carry

    lax.fori_loop(0, UNITS, drain, 0)
    for copy in lead_copies:
        copy.wait_send()
    for image in range(2):
        norm_copy(image).wait_send()
    for image in range(IMAGES):
        part_copy(image).wait_send()
    for group in range(2):
        for hop in range(1, RING):
            for step in range(RING):
                first_copy(group, hop, step).wait_send()
        for hop in range(RING):
            for step in range(1, RING):
                last_copy(group, hop, step, group).wait_send()
                last_copy(group, hop, step, group).wait_recv()

            @pl.when(group != gy)
            def _():
                last_copy(group, hop, 0, group).wait_send()
                last_copy(group, hop, 0, group).wait_recv()

            @pl.when(group == gy)
            def _():
                stay_copy(group, hop, group).wait()


def on_device(x_in, ln_gain, w_qkv, q_gain, k_gain, w_out, counts, dest):
    any_spec = pl.BlockSpec(memory_space=pl.ANY)
    dma = pltpu.SemaphoreType.DMA
    routed = pl.pallas_call(
        kernel,
        out_shape=pltpu.VMEM((RING, RING, CAP, BLOCK), BF16),
        in_specs=[any_spec] * 8,
        out_specs=any_spec,
        scratch_shapes=[
            pltpu.VMEM((2 * PATCHES, BLOCK), BF16),
            pltpu.VMEM((BLOCK,), F32),
            pltpu.VMEM((1, 128), F32),
            pltpu.VMEM((1, 128), F32),
            pltpu.SMEM((2, 8), jnp.int32),
            pltpu.SMEM((2, 8), jnp.int32),
            pltpu.VMEM((2, 2 * PATCHES, WIDE), BF16),
            pltpu.VMEM((IMAGES, PATCHES, BLOCK), BF16),
            pltpu.VMEM((4, SLOTS, BLOCK, GROUP), BF16),
            pltpu.VMEM((2, SLOTS, 4 * 128, WIDE), BF16),
            pltpu.VMEM((UNITS, PATCHES, GROUP), BF16),
            pltpu.VMEM((UNITS, PATCHES, GROUP), BF16),
            pltpu.VMEM((UNITS, PATCHES, GROUP), BF16),
            pltpu.VMEM((UNITS, HALF, GROUP), BF16),
            pltpu.VMEM((UNITS, HALF, GROUP), BF16),
            pltpu.VMEM((UNITS, PATCHES, GROUP), BF16),
            pltpu.VMEM((UNITS, PATCHES, GROUP), BF16),
            pltpu.VMEM((UNITS, PATCHES, 4 * 128), BF16),
            pltpu.VMEM((PATCHES, GROUP), F32),
            pltpu.VMEM((PATCHES + 16, BLOCK), BF16),
            pltpu.VMEM((PATCHES, 128), F32),
            pltpu.VMEM((4, 8, GROUP), F32),
            pltpu.VMEM((3, 8, GROUP), F32),
            pltpu.VMEM((IMAGES, PATCHES, WIDE), BF16),
            pltpu.VMEM((IMAGES, PATCHES, WIDE), BF16),
            pltpu.VMEM((IMAGES, PATCHES, WIDE), BF16),
            pltpu.VMEM((2 * PATCHES, WIDE), BF16),
            pltpu.VMEM((RING, RING * CAP, 2 * PATCHES), BF16),
            pltpu.VMEM((2, RING - 1, RING, CAP, WIDE), BF16),
            pltpu.VMEM((2, RING, RING, CAP, WIDE), BF16),
            pltpu.VMEM((2, 8, 2 * PATCHES), jnp.int32),
            pltpu.VMEM((2, 8, PATCHES), F32),
            pltpu.VMEM((2, 3, 8, PATCHES), F32),
            dma((2,)),
            dma((5,)),
            dma(()),
            dma((4, SLOTS, 3)),
            dma((2, SLOTS, 4)),
            dma(()),
            dma(()),
            dma(()),
            dma(()),
            dma((2, 3)),
            dma((2, 3)),
            dma((3,)),
            dma((3,)),
            dma((2,)),
            dma((2,)),
            dma((UNITS, 6)),
            dma((UNITS, 6)),
            dma((UNITS, 4)),
            dma((UNITS, 4)),
            dma((IMAGES,)),
            dma((IMAGES,)),
            dma((2, RING - 1, RING)),
            dma((2, RING - 1, RING)),
            dma((2, RING, RING)),
            dma((2, RING, RING)),
            dma((RING,)),
        ],
        compiler_params=pltpu.CompilerParams(
            collective_id=0, has_side_effects=True, vmem_limit_bytes=58 * 2**20
        ),
        cost_estimate=pl.CostEstimate(
            flops=20 * 10**9, bytes_accessed=25 * 10**6, transcendentals=10**6
        ),
        name="layer",
    )(
        x_in.reshape(2 * PATCHES, BLOCK),
        ln_gain,
        jnp.transpose(w_qkv, (1, 2, 0, 3)),
        q_gain.reshape(1, 128),
        k_gain.reshape(1, 128),
        w_out.reshape(BLOCK, BLOCK),
        counts,
        dest,
    )
    return routed.reshape(1, 1, RANKS, 1, CAP, BLOCK)


def solution(mesh):
    in_specs = (
        P(("gy", "gz"), None, "gx"),
        P("gx"),
        P("gx", "gy", None, None),
        P(),
        P(),
        P("gy", None, "gx"),
        P(("gy", "gz"), None),
        P(("gy", "gz"), None),
    )
    out_specs = P("gy", "gz", None, None, None, "gx")
    return jax.shard_map(
        on_device, mesh=mesh, in_specs=in_specs, out_specs=out_specs, check_vma=False
    )
```

```python
import functools
import math

import jax
import jax.numpy as jnp
from jax import lax
from jax.experimental import pallas as pl
from jax.experimental.pallas import tpu as pltpu
from jax.sharding import PartitionSpec as P

D = 6144
PATCHES = 256
HALF = PATCHES // 2
BLOCK = 1536
WIDE = BLOCK // 2
GROUP = 384
SLOTS = 3
RANKS = 16
RING = 4
CAP = 64
IMAGES = 4
UNITS = IMAGES * SLOTS
EPS = 1e-06
MESH = pl.DeviceIdType.MESH
BF16 = jnp.bfloat16
F32 = jnp.float32

OPP, RIGHT, LEFT, OWN = 0, 1, 2, 3
TWO_RIGHT, TWO_LEFT, RIGHT_HIGH, LEFT_LOW, RIGHT_LOW, LEFT_HIGH = range(6)
ATT_RIGHT, ATT_LEFT, PASS_RIGHT, PASS_LEFT = range(4)
LOW = pl.ds(0, HALF)
HIGH = pl.ds(HALF, HALF)


def head_norm(values, gain):
    mean_value = jnp.mean(values, axis=-1, keepdims=True)
    spread = jnp.mean(values * values, axis=-1, keepdims=True) - mean_value * mean_value
    return ((values - mean_value) * lax.rsqrt(spread + EPS) * gain).astype(BF16)


def remote(src, dst, send_sem, recv_sem, device):
    return pltpu.make_async_remote_copy(
        src_ref=src,
        dst_ref=dst,
        send_sem=send_sem,
        recv_sem=recv_sem,
        device_id=device,
        device_id_type=MESH,
    )


def kernel(
    x_hbm, gain_hbm, wq_hbm, q_gain_hbm, k_gain_hbm, wo_hbm, counts_hbm, dest_hbm,
    out_hbm,
    x_ref, gain_ref, q_gain_ref, k_gain_ref, counts_ref, dest_ref, x_half, normed, wq, wo, two, to_right, to_left, from_two_left, from_two_right,
    from_left, from_right, attended, held, lead, fix, lead_out, lead_in, mine, leaving, other, layer, picks, outgoing, middle, target,
    stats, stats_in,
    x_sem, small_sem, half_sem, wq_sem, wo_sem, half_send, half_recv, target_send, target_recv,
    stat_send, stat_recv, lead_send, lead_recv, norm_send, norm_recv, sum_send, sum_recv, att_send, att_recv,
    part_send, part_recv, first_send, first_recv, last_send, last_recv, local_sem,
):
    gx, gy, gz = lax.axis_index("gx"), lax.axis_index("gy"), lax.axis_index("gz")
    at = {
        OPP: lax.rem(gx + 2, RING),
        RIGHT: lax.rem(gx + 1, RING),
        LEFT: lax.rem(gx + 3, RING),
        OWN: gx,
    }
    line = {role: (at[role], gy, gz) for role in (OPP, RIGHT, LEFT)}
    sibling = (gx, 1 - gy, gz)
    z_at, y_at = lax.div(gz, RING), lax.rem(gz, RING)
    first_at = (1 - gy) * y_at + gy * z_at
    last_at = (1 - gy) * z_at + gy * y_at

    def plane(first, last):
        return first * (1 + 3 * gy) + last * (4 - 3 * gy)

    def on_first(step):
        return plane(lax.rem(first_at + step, RING), last_at)

    def on_last(step):
        return plane(first_at, lax.rem(last_at + step, RING))

    rows_of = [pl.ds(image * PATCHES, PATCHES) for image in range(2)]
    x_copies = [
        pltpu.make_async_copy(x_hbm.at[rows], x_ref.at[rows], x_sem.at[image])
        for image, rows in enumerate(rows_of)
    ]
    x_copies[0].start()

    barrier = pltpu.get_barrier_semaphore()
    partners = [line[OPP], line[RIGHT], line[LEFT], sibling]
    for step in range(1, RING):
        partners.append((gx, gy, on_first(step)))
        partners.append((gx, gy, on_last(step)))
        partners.append((gx, 1 - gy, on_first(step)))
    for partner in partners:
        pl.semaphore_signal(barrier, inc=1, device_id=partner, device_id_type=MESH)

    small_copies = [
        pltpu.make_async_copy(src, dst, small_sem.at[k])
        for k, (src, dst) in enumerate((
            (gain_hbm, gain_ref), (q_gain_hbm, q_gain_ref), (k_gain_hbm, k_gain_ref),
            (counts_hbm, counts_ref), (dest_hbm, dest_ref),
        ))
    ]
    for copy in small_copies:
        copy.start()
    x_copies[1].start()

    def wq_copies(role, slot):
        return [
            pltpu.make_async_copy(
                wq_hbm.at[at[role] * SLOTS + slot, k],
                wq.at[role, slot, :, pl.ds(k * 128, 128)],
                wq_sem.at[role, slot, k],
            )
            for k in range(3)
        ]

    def wo_copies():
        for side in range(2):
            core = gy if side == 1 else 1 - gy
            for slot in range(SLOTS):
                for role in (OPP, RIGHT, LEFT, OWN):
                    row = pl.multiple_of((at[role] * SLOTS + slot) * 128, 128)
                    yield pltpu.make_async_copy(
                        wo_hbm.at[pl.ds(row, 128), pl.ds(pl.multiple_of(core * WIDE, WIDE), WIDE)],
                        wo.at[side, slot, pl.ds(role * 128, 128)],
                        wo_sem.at[side, slot, role],
                    )

    half_copy = pltpu.make_async_copy(
        x_hbm.at[:, pl.ds(pl.multiple_of(gy * WIDE, WIDE), WIDE)], x_half.at[gy], half_sem
    )

    def wait_weights(role, slot):
        for copy in wq_copies(role, slot):
            copy.wait()

    for role in (OPP, RIGHT, LEFT):
        for copy in wq_copies(role, 0):
            copy.start()
    def sum_copy(unit, kind):
        src, dst, role = {
            TWO_RIGHT: (two.at[unit, LOW], from_two_left.at[unit], RIGHT),
            TWO_LEFT: (two.at[unit, HIGH], from_two_right.at[unit], LEFT),
            RIGHT_HIGH: (to_right.at[unit, HIGH], from_left.at[unit, HIGH], RIGHT),
            LEFT_LOW: (to_left.at[unit, LOW], from_right.at[unit, LOW], LEFT),
            RIGHT_LOW: (to_right.at[unit, LOW], from_left.at[unit, LOW], RIGHT),
            LEFT_HIGH: (to_left.at[unit, HIGH], from_right.at[unit, HIGH], LEFT),
        }[kind]
        return remote(src, dst, sum_send.at[unit, kind], sum_recv.at[unit, kind], line[role])

    lane = lax.broadcasted_iota(jnp.int32, (PATCHES, 128), 1)
    mirror = {OPP: OPP, RIGHT: LEFT, LEFT: RIGHT}

    def stat_copies(image):
        return [
            remote(
                stats.at[image], stats_in.at[image, mirror[role]], stat_send.at[image, role],
                stat_recv.at[image, mirror[role]], line[role],
            )
            for role in (OPP, RIGHT, LEFT)
        ]

    def add_up(image):
        x_copies[image].wait()
        xf = x_ref[rows_of[image], :].astype(F32)
        sums = jnp.sum(xf, axis=-1, keepdims=True)
        both = jnp.where(lane == 0, sums, jnp.sum(xf * xf, axis=-1, keepdims=True))
        stats[image] = jnp.transpose(both)[0:8, :]
        return xf, sums

    for copy in small_copies:
        copy.wait()
    gain = gain_ref[...].reshape(1, BLOCK)
    xf, sums = add_up(0)
    lead[pl.ds(0, PATCHES), :] = ((xf - sums * (1.0 / BLOCK)) * gain).astype(BF16)
    high = gain.astype(BF16).astype(F32)
    line_at = lax.broadcasted_iota(jnp.int32, (16, BLOCK), 0)
    lead[pl.ds(PATCHES, 16), :] = jnp.where(
        line_at == 0, high, jnp.where(line_at == 1, gain - high, 0.0)
    ).astype(BF16)

    first_unit = 2 * SLOTS * gy

    def lead_product(role):
        full = jnp.dot(lead[...], wq[role, 0], preferred_element_type=F32)
        lead_out[role] = jnp.broadcast_to(
            full[PATCHES:PATCHES + 1, :] + full[PATCHES + 1:PATCHES + 2, :], (8, GROUP)
        )
        return full[0:PATCHES, :]

    lead_copies = [
        remote(
            lead_out.at[role], lead_in.at[mirror[role]], lead_send.at[role],
            lead_recv.at[mirror[role]], line[role],
        )
        for role in (OPP, RIGHT, LEFT)
    ]

    wait_weights(OPP, 0)
    two[first_unit] = lead_product(OPP).astype(BF16)
    for slot in range(SLOTS):
        for role in (OPP, RIGHT, LEFT, OWN):
            if slot != 0 or role == OWN:
                for copy in wq_copies(role, slot):
                    copy.start()

    pl.semaphore_wait(barrier, len(partners))

    for copy in stat_copies(0):
        copy.start()
    sum_copy(first_unit, TWO_RIGHT).start()
    sum_copy(first_unit, TWO_LEFT).start()
    wait_weights(RIGHT, 0)
    to_right[first_unit] = lead_product(RIGHT).astype(BF16)
    sum_copy(first_unit, RIGHT_HIGH).start()
    wait_weights(LEFT, 0)
    to_left[first_unit] = lead_product(LEFT).astype(BF16)
    sum_copy(first_unit, LEFT_LOW).start()
    add_up(1)
    for copy in stat_copies(1):
        copy.start()
    for copy in lead_copies:
        copy.start()

    def norm_copy(image):
        moved = normed.at[gy * 2 + image]
        return remote(moved, moved, norm_send.at[image], norm_recv.at[image], sibling)

    def normalize(image):
        for copy in stat_copies(image):
            copy.wait()
        shares = [stats_in[image, OPP], stats_in[image, RIGHT], stats_in[image, LEFT], stats[image]]
        total = shares[0] + shares[1] + shares[2] + shares[3]
        line_at = lax.broadcasted_iota(jnp.int32, (8, PATCHES), 0)
        part = jnp.where(line_at == 5, total[1:2, :], 0.0)
        for k, share in enumerate(shares + [total]):
            part = jnp.where(line_at == k, share[0:1, :], part)
        column = jnp.transpose(jnp.concatenate([part] * 16, axis=0))
        mean_value = column[:, 4:5] * (1.0 / D)
        spread = column[:, 5:6] * (1.0 / D) - mean_value * mean_value
        scale = lax.rsqrt(spread + EPS)
        if image == 0:
            fix[...] = jnp.where(lane == 4, scale, column * (1.0 / BLOCK) - mean_value)
        xf = x_ref[rows_of[image], :].astype(F32)
        normed[gy * 2 + image] = (
            (xf - mean_value) * scale * gain_ref[...].reshape(1, BLOCK)
        ).astype(BF16)
        norm_copy(image).start()

    def att_copy(unit, kind):
        every = pl.ds(0, PATCHES)
        rows, source, place, role = {
            ATT_RIGHT: (every, OWN, LEFT, RIGHT),
            ATT_LEFT: (every, OWN, RIGHT, LEFT),
            PASS_RIGHT: (LOW, LEFT, OPP, RIGHT),
            PASS_LEFT: (HIGH, RIGHT, OPP, LEFT),
        }[kind]
        return remote(
            attended.at[unit, rows, pl.ds(source * 128, 128)],
            attended.at[unit, rows, pl.ds(place * 128, 128)],
            att_send.at[unit, kind], att_recv.at[unit, kind], line[role],
        )

    def part_copy(image):
        return remote(
            leaving.at[image], other.at[image], part_send.at[image], part_recv.at[image], sibling
        )

    def first_copy(group, hop, step):
        to = lax.rem(last_at + step, RING)
        return remote(
            outgoing.at[group, hop - 1, to], middle.at[group, to, first_at],
            first_send.at[group, hop - 1, step], first_recv.at[group, hop - 1, step],
            (gx, gy, on_first(hop)),
        )

    columns = {core: pl.ds(core * WIDE, WIDE) for core in range(2)}

    def landing(core, source):
        if core == 0:
            return out_hbm.at[last_at, source, :, columns[core]]
        return out_hbm.at[source, last_at, :, columns[core]]

    def last_copy(group, hop, step, core):
        source = lax.rem(first_at + RING - hop, RING)
        return remote(
            middle.at[group, lax.rem(last_at + step, RING), source], landing(core, source),
            last_send.at[group, hop, step], last_recv.at[core, hop, step],
            (gx, group, on_last(step)),
        )

    def stay_copy(group, hop, core):
        source = lax.rem(first_at + RING - hop, RING)
        return pltpu.make_async_copy(
            middle.at[group, last_at, source], landing(core, source), local_sem.at[hop]
        )

    def product(unit, role):
        return jnp.dot(
            normed[lax.div(unit, SLOTS)], wq[role, lax.rem(unit, SLOTS)],
            preferred_element_type=F32,
        )

    def mend(values):
        for role in (OPP, RIGHT, LEFT):
            values = values + fix[:, role:role + 1] * lead_in[role][0:1, :]
        return fix[:, 4:5] * (values + fix[:, OWN:OWN + 1] * lead_out[OWN][0:1, :])

    def attend(unit, is_first):
        @pl.when(is_first)
        def _():
            held[...] = lead_product(OWN)
            for copy in lead_copies:
                copy.wait_recv()

        @pl.when(jnp.logical_not(is_first))
        def _():
            held[...] = product(unit, OWN)

        for kind in (RIGHT_HIGH, LEFT_LOW, RIGHT_LOW, LEFT_HIGH):
            sum_copy(unit, kind).wait_recv()
        held[...] += from_left[unit].astype(F32) + from_right[unit].astype(F32)

        @pl.when(is_first)
        def _():
            held[...] = mend(held[...])

        qkv = held[...]
        query = head_norm(qkv[:, 0:128], q_gain_ref[...])
        keys = head_norm(qkv[:, 128:256], k_gain_ref[...])
        values = qkv[:, 256:384].astype(BF16)
        scores = lax.dot_general(
            query, keys, (((1,), (1,)), ((), ())), preferred_element_type=F32
        ) * (1.0 / math.sqrt(128))
        expo = jnp.exp(scores)
        weights = (expo * (1.0 / jnp.sum(expo, axis=-1, keepdims=True))).astype(BF16)
        attended[unit, :, pl.ds(OWN * 128, 128)] = jnp.dot(
            weights, values, preferred_element_type=F32
        ).astype(BF16)
        att_copy(unit, ATT_RIGHT).start()
        att_copy(unit, ATT_LEFT).start()

    def project(image, side, slots):
        parts = [
            jnp.dot(attended[image * SLOTS + slot], wo[side, slot], preferred_element_type=F32)
            for slot in slots
        ]
        return parts[0] if len(parts) == 1 else parts[0] + parts[1]

    def send_last(group, hop, step):
        for core in range(2):
            @pl.when(gy == core)
            def _():
                if step != 0:
                    last_copy(group, hop, step, core).start()
                else:
                    @pl.when(group == gy)
                    def _():
                        stay_copy(group, hop, core).start()

                    @pl.when(group != gy)
                    def _():
                        last_copy(group, hop, 0, core).start()

    def route_on(group):
        for hop in (1, 3, 2):
            for step in (2, 1, 3):
                first_copy(group, hop, step).wait_recv()
                send_last(group, hop, step)
        for hop in range(1, RING):
            first_copy(group, hop, 0).wait_recv()
            send_last(group, hop, 0)

    def finish(held_image):
        part_copy(held_image).wait_recv()
        rows = pl.ds(pl.multiple_of(lax.rem(held_image, 2) * PATCHES, PATCHES), PATCHES)
        layer[rows, :] = (
            x_half[lax.div(held_image, 2), rows, :].astype(F32)
            + (mine[held_image].astype(F32) + other[held_image].astype(F32))
        ).astype(BF16)

    def prepare(group):
        finish(2 * group)
        place = lax.broadcasted_iota(jnp.int32, (RING * CAP, 1), 0)
        places = target[group][0:1, :]
        for step in range(RING):
            rank = plane(lax.rem(first_at + step, RING), place >> 6)
            picks[step] = jnp.where(
                rank * CAP + (place & (CAP - 1)) == places, 1.0, 0.0
            ).astype(BF16)

    def route(group):
        finish(2 * group + 1)
        for step in (1, 3, 2, 0):
            picked = jnp.dot(picks[step], layer[...], preferred_element_type=F32).astype(BF16)
            picked = picked.reshape(RING, CAP, WIDE)
            if step == 0:
                for to in range(RING):
                    middle[group, to, first_at] = picked[to]
            else:
                outgoing[group, step - 1] = picked
                for on in (2, 1, 3):
                    first_copy(group, step, on).start()
        for step in (1, 3, 2):
            first_copy(group, step, 0).start()
        for on in (2, 1, 3, 0):
            send_last(group, 0, on)

    def towards_opposite(unit):
        two[unit] = product(unit, OPP).astype(BF16)
        sum_copy(unit, TWO_RIGHT).start()
        sum_copy(unit, TWO_LEFT).start()

    normalize(0)
    sum_copy(first_unit, TWO_RIGHT).wait_recv()
    to_right[first_unit, LOW, :] = (
        to_right[first_unit, LOW, :].astype(F32) + from_two_left[first_unit].astype(F32)
    ).astype(BF16)
    sum_copy(first_unit, RIGHT_LOW).start()
    sum_copy(first_unit, TWO_LEFT).wait_recv()
    to_left[first_unit, HIGH, :] = (
        to_left[first_unit, HIGH, :].astype(F32) + from_two_right[first_unit].astype(F32)
    ).astype(BF16)
    sum_copy(first_unit, LEFT_HIGH).start()
    wait_weights(OPP, 1)

    @pl.when(gy == 0)
    def _():
        towards_opposite(1)

    normalize(1)

    @pl.when(gy == 1)
    def _():
        norm_copy(0).wait_recv()
        towards_opposite(0)

    row = lax.broadcasted_iota(jnp.int32, (8, 2 * PATCHES), 1)
    places = jnp.full((8, 2 * PATCHES), RANKS * CAP, jnp.int32)
    for image in range(2):
        begin = image * PATCHES
        for piece in range(8):
            stop = begin + counts_ref[image, piece]
            places = jnp.where(
                (row >= begin) & (row < stop), dest_ref[image, piece] * CAP + row - begin, places
            )
            begin = stop
    target[gy] = places
    target_copy = remote(target.at[gy], target.at[gy], target_send, target_recv, sibling)
    target_copy.start()
    cross_copy = remote(
        x_hbm.at[:, pl.ds(pl.multiple_of((1 - gy) * WIDE, WIDE), WIDE)],
        x_half.at[gy], half_send, half_recv, sibling,
    )
    cross_copy.start()
    half_copy.start()
    for copy in wo_copies():
        copy.start()

    def turn(step, carry):
        def back(count):
            at_turn = lax.rem(step + UNITS - count, UNITS)
            late = lax.div(at_turn, 2 * SLOTS + 1)
            shifted = lax.rem(at_turn + 2 * SLOTS, 2 * SLOTS + 1)
            return (1 - gy) * at_turn + gy * (late * at_turn + (1 - late) * shifted)

        @pl.when((step == 9) | (step == 14))
        def _():
            prepare(lax.div(step, 14))

        @pl.when((step >= 2) & (step <= UNITS))
        def _():
            unit = back(1)

            @pl.when(step <= SLOTS)
            def _():
                wait_weights(RIGHT, lax.rem(step + 2, SLOTS))
                wait_weights(LEFT, lax.rem(step + 2, SLOTS))

            mine_right = product(unit, RIGHT)
            to_right[unit, HIGH, :] = mine_right[HALF:, :].astype(BF16)
            sum_copy(unit, RIGHT_HIGH).start()
            sum_copy(unit, TWO_RIGHT).wait_recv()
            to_right[unit, LOW, :] = (
                mine_right[:HALF, :] + from_two_left[unit].astype(F32)
            ).astype(BF16)
            sum_copy(unit, RIGHT_LOW).start()
            mine_left = product(unit, LEFT)
            to_left[unit, LOW, :] = mine_left[:HALF, :].astype(BF16)
            sum_copy(unit, LEFT_LOW).start()
            sum_copy(unit, TWO_LEFT).wait_recv()
            to_left[unit, HIGH, :] = (
                mine_left[HALF:, :] + from_two_right[unit].astype(F32)
            ).astype(BF16)
            sum_copy(unit, LEFT_HIGH).start()

        @pl.when((step >= 1) & (step <= UNITS - 2))
        def _():
            unit = back(-1)
            image = lax.div(unit, SLOTS)

            @pl.when((lax.rem(unit, SLOTS) == 0) & (lax.div(image, 2) != gy))
            def _():
                norm_copy(lax.rem(image, 2)).wait_recv()

            @pl.when(step == 1)
            def _():
                wait_weights(OPP, 2)

            towards_opposite(unit)

        @pl.when((step >= 2) & (step <= UNITS + 1))
        def _():
            unit = back(2)

            @pl.when(step < SLOTS + 2)
            def _():
                wait_weights(OWN, lax.rem(step + 1, SLOTS))

            attend(unit, step == 2)

        @pl.when((step >= 3) & (step <= UNITS + 2))
        def _():
            unit = back(3)
            att_copy(unit, ATT_RIGHT).wait_recv()
            att_copy(unit, PASS_RIGHT).start()
            att_copy(unit, ATT_LEFT).wait_recv()
            att_copy(unit, PASS_LEFT).start()

        @pl.when((step == 7) | (step == 10) | (step == 13) | (step == 16))
        def _():
            image = lax.div(step, 3) - 2

            @pl.when(step == 7)
            def _():
                for copy in wo_copies():
                    copy.wait()
                half_copy.wait()
                target_copy.wait()
                cross_copy.wait()

            def wait_slot(slot):
                att_copy(image * SLOTS + slot, PASS_RIGHT).wait_recv()
                att_copy(image * SLOTS + slot, PASS_LEFT).wait_recv()

            wait_slot(0)
            wait_slot(1)
            early = [project(image, side, (0, 1)) for side in range(2)]
            wait_slot(2)
            leaving[image] = (early[0] + project(image, 0, (2,))).astype(BF16)
            part_copy(image).start()
            mine[image] = (early[1] + project(image, 1, (2,))).astype(BF16)

        @pl.when((step == 10) | (step == 16))
        def _():
            route(lax.div(step, 16))

        @pl.when((step == 12) | (step == 17))
        def _():
            route_on(lax.div(step, 17))

        return carry

    lax.fori_loop(1, UNITS + 6, turn, 0)

    def drain(unit, carry):
        for kind in range(6):
            sum_copy(unit, kind).wait_send()
        for kind in range(4):
            att_copy(unit, kind).wait_send()
        return carry

    lax.fori_loop(0, UNITS, drain, 0)
    for copy in lead_copies:
        copy.wait_send()
    for image in range(2):
        norm_copy(image).wait_send()
    for image in range(IMAGES):
        part_copy(image).wait_send()
    for group in range(2):
        for hop in range(1, RING):
            for step in range(RING):
                first_copy(group, hop, step).wait_send()
        for hop in range(RING):
            for step in range(1, RING):
                last_copy(group, hop, step, group).wait_send()
                last_copy(group, hop, step, group).wait_recv()

            @pl.when(group != gy)
            def _():
                last_copy(group, hop, 0, group).wait_send()
                last_copy(group, hop, 0, group).wait_recv()

            @pl.when(group == gy)
            def _():
                stay_copy(group, hop, group).wait()


def on_device(x_in, ln_gain, w_qkv, q_gain, k_gain, w_out, counts, dest):
    any_spec = pl.BlockSpec(memory_space=pl.ANY)
    dma = pltpu.SemaphoreType.DMA
    routed = pl.pallas_call(
        kernel,
        out_shape=pltpu.VMEM((RING, RING, CAP, BLOCK), BF16),
        in_specs=[any_spec] * 8,
        out_specs=any_spec,
        scratch_shapes=[
            pltpu.VMEM((2 * PATCHES, BLOCK), BF16),
            pltpu.VMEM((BLOCK,), F32),
            pltpu.VMEM((1, 128), F32),
            pltpu.VMEM((1, 128), F32),
            pltpu.SMEM((2, 8), jnp.int32),
            pltpu.SMEM((2, 8), jnp.int32),
            pltpu.VMEM((2, 2 * PATCHES, WIDE), BF16),
            pltpu.VMEM((IMAGES, PATCHES, BLOCK), BF16),
            pltpu.VMEM((4, SLOTS, BLOCK, GROUP), BF16),
            pltpu.VMEM((2, SLOTS, 4 * 128, WIDE), BF16),
            pltpu.VMEM((UNITS, PATCHES, GROUP), BF16),
            pltpu.VMEM((UNITS, PATCHES, GROUP), BF16),
            pltpu.VMEM((UNITS, PATCHES, GROUP), BF16),
            pltpu.VMEM((UNITS, HALF, GROUP), BF16),
            pltpu.VMEM((UNITS, HALF, GROUP), BF16),
            pltpu.VMEM((UNITS, PATCHES, GROUP), BF16),
            pltpu.VMEM((UNITS, PATCHES, GROUP), BF16),
            pltpu.VMEM((UNITS, PATCHES, 4 * 128), BF16),
            pltpu.VMEM((PATCHES, GROUP), F32),
            pltpu.VMEM((PATCHES + 16, BLOCK), BF16),
            pltpu.VMEM((PATCHES, 128), F32),
            pltpu.VMEM((4, 8, GROUP), F32),
            pltpu.VMEM((3, 8, GROUP), F32),
            pltpu.VMEM((IMAGES, PATCHES, WIDE), BF16),
            pltpu.VMEM((IMAGES, PATCHES, WIDE), BF16),
            pltpu.VMEM((IMAGES, PATCHES, WIDE), BF16),
            pltpu.VMEM((2 * PATCHES, WIDE), BF16),
            pltpu.VMEM((RING, RING * CAP, 2 * PATCHES), BF16),
            pltpu.VMEM((2, RING - 1, RING, CAP, WIDE), BF16),
            pltpu.VMEM((2, RING, RING, CAP, WIDE), BF16),
            pltpu.VMEM((2, 8, 2 * PATCHES), jnp.int32),
            pltpu.VMEM((2, 8, PATCHES), F32),
            pltpu.VMEM((2, 3, 8, PATCHES), F32),
            dma((2,)),
            dma((5,)),
            dma(()),
            dma((4, SLOTS, 3)),
            dma((2, SLOTS, 4)),
            dma(()),
            dma(()),
            dma(()),
            dma(()),
            dma((2, 3)),
            dma((2, 3)),
            dma((3,)),
            dma((3,)),
            dma((2,)),
            dma((2,)),
            dma((UNITS, 6)),
            dma((UNITS, 6)),
            dma((UNITS, 4)),
            dma((UNITS, 4)),
            dma((IMAGES,)),
            dma((IMAGES,)),
            dma((2, RING - 1, RING)),
            dma((2, RING - 1, RING)),
            dma((2, RING, RING)),
            dma((2, RING, RING)),
            dma((RING,)),
        ],
        compiler_params=pltpu.CompilerParams(
            collective_id=0, has_side_effects=True, vmem_limit_bytes=58 * 2**20
        ),
        cost_estimate=pl.CostEstimate(
            flops=20 * 10**9, bytes_accessed=25 * 10**6, transcendentals=10**6
        ),
        name="layer",
    )(
        x_in.reshape(2 * PATCHES, BLOCK),
        ln_gain,
        jnp.transpose(w_qkv, (1, 2, 0, 3)),
        q_gain.reshape(1, 128),
        k_gain.reshape(1, 128),
        w_out.reshape(BLOCK, BLOCK),
        counts,
        dest,
    )
    return routed.reshape(1, 1, RANKS, 1, CAP, BLOCK)


def solution(mesh):
    in_specs = (
        P(("gy", "gz"), None, "gx"),
        P("gx"),
        P("gx", "gy", None, None),
        P(),
        P(),
        P("gy", None, "gx"),
        P(("gy", "gz"), None),
        P(("gy", "gz"), None),
    )
    out_specs = P("gy", "gz", None, None, None, "gx")
    return jax.shard_map(
        on_device, mesh=mesh, in_specs=in_specs, out_specs=out_specs, check_vma=False
    )
```

```python
import functools
import math

import jax
import jax.numpy as jnp
from jax import lax
from jax.experimental import pallas as pl
from jax.experimental.pallas import tpu as pltpu
from jax.sharding import PartitionSpec as P

D = 6144
PATCHES = 256
HALF = PATCHES // 2
BLOCK = 1536
WIDE = BLOCK // 2
GROUP = 384
SLOTS = 3
RANKS = 16
RING = 4
CAP = 64
IMAGES = 4
UNITS = IMAGES * SLOTS
EPS = 1e-06
MESH = pl.DeviceIdType.MESH
BF16 = jnp.bfloat16
F32 = jnp.float32

OPP, RIGHT, LEFT, OWN = 0, 1, 2, 3
TWO_RIGHT, TWO_LEFT, RIGHT_HIGH, LEFT_LOW, RIGHT_LOW, LEFT_HIGH = range(6)
ATT_RIGHT, ATT_LEFT, PASS_RIGHT, PASS_LEFT = range(4)
LOW = pl.ds(0, HALF)
HIGH = pl.ds(HALF, HALF)


def head_norm(values, gain):
    mean_value = jnp.mean(values, axis=-1, keepdims=True)
    spread = jnp.mean(values * values, axis=-1, keepdims=True) - mean_value * mean_value
    return ((values - mean_value) * lax.rsqrt(spread + EPS) * gain).astype(BF16)


def remote(src, dst, send_sem, recv_sem, device):
    return pltpu.make_async_remote_copy(
        src_ref=src,
        dst_ref=dst,
        send_sem=send_sem,
        recv_sem=recv_sem,
        device_id=device,
        device_id_type=MESH,
    )


def kernel(
    x_hbm, gain_hbm, wq_hbm, q_gain_hbm, k_gain_hbm, wo_hbm, counts_hbm, dest_hbm,
    out_hbm,
    x_ref, gain_ref, q_gain_ref, k_gain_ref, counts_ref, dest_ref, x_half, normed, wq, wo, two, to_right, to_left, from_two_left, from_two_right,
    from_left, from_right, attended, held, lead, fix, lead_out, lead_in, mine, leaving, other, layer, picks, outgoing, middle, target,
    stats, stats_in,
    x_sem, small_sem, half_sem, wq_sem, wo_sem, half_send, half_recv, target_send, target_recv,
    stat_send, stat_recv, lead_send, lead_recv, norm_send, norm_recv, sum_send, sum_recv, att_send, att_recv,
    part_send, part_recv, first_send, first_recv, last_send, last_recv, local_sem,
):
    gx, gy, gz = lax.axis_index("gx"), lax.axis_index("gy"), lax.axis_index("gz")
    at = {
        OPP: lax.rem(gx + 2, RING),
        RIGHT: lax.rem(gx + 1, RING),
        LEFT: lax.rem(gx + 3, RING),
        OWN: gx,
    }
    line = {role: (at[role], gy, gz) for role in (OPP, RIGHT, LEFT)}
    sibling = (gx, 1 - gy, gz)
    z_at, y_at = lax.div(gz, RING), lax.rem(gz, RING)
    first_at = (1 - gy) * y_at + gy * z_at
    last_at = (1 - gy) * z_at + gy * y_at

    def plane(first, last):
        return first * (1 + 3 * gy) + last * (4 - 3 * gy)

    def on_first(step):
        return plane(lax.rem(first_at + step, RING), last_at)

    def on_last(step):
        return plane(first_at, lax.rem(last_at + step, RING))

    rows_of = [pl.ds(image * PATCHES, PATCHES) for image in range(2)]
    x_copies = [
        pltpu.make_async_copy(x_hbm.at[rows], x_ref.at[rows], x_sem.at[image])
        for image, rows in enumerate(rows_of)
    ]
    x_copies[0].start()

    barrier = pltpu.get_barrier_semaphore()
    partners = [line[OPP], line[RIGHT], line[LEFT], sibling]
    for step in range(1, RING):
        partners.append((gx, gy, on_first(step)))
        partners.append((gx, gy, on_last(step)))
        partners.append((gx, 1 - gy, on_first(step)))
    for partner in partners:
        pl.semaphore_signal(barrier, inc=1, device_id=partner, device_id_type=MESH)

    small_copies = [
        pltpu.make_async_copy(src, dst, small_sem.at[k])
        for k, (src, dst) in enumerate((
            (gain_hbm, gain_ref), (q_gain_hbm, q_gain_ref), (k_gain_hbm, k_gain_ref),
            (counts_hbm, counts_ref), (dest_hbm, dest_ref),
        ))
    ]
    for copy in small_copies:
        copy.start()
    x_copies[1].start()

    def wq_copies(role, slot):
        return [
            pltpu.make_async_copy(
                wq_hbm.at[at[role] * SLOTS + slot, k],
                wq.at[role, slot, :, pl.ds(k * 128, 128)],
                wq_sem.at[role, slot, k],
            )
            for k in range(3)
        ]

    def wo_copies():
        for side in range(2):
            core = gy if side == 1 else 1 - gy
            for slot in range(SLOTS):
                for role in (OPP, RIGHT, LEFT, OWN):
                    row = pl.multiple_of((at[role] * SLOTS + slot) * 128, 128)
                    yield pltpu.make_async_copy(
                        wo_hbm.at[pl.ds(row, 128), pl.ds(pl.multiple_of(core * WIDE, WIDE), WIDE)],
                        wo.at[side, slot, pl.ds(role * 128, 128)],
                        wo_sem.at[side, slot, role],
                    )

    half_copy = pltpu.make_async_copy(
        x_hbm.at[:, pl.ds(pl.multiple_of(gy * WIDE, WIDE), WIDE)], x_half.at[gy], half_sem
    )

    def wait_weights(role, slot):
        for copy in wq_copies(role, slot):
            copy.wait()

    for role in (OPP, RIGHT, LEFT):
        for copy in wq_copies(role, 0):
            copy.start()
    def sum_copy(unit, kind):
        src, dst, role = {
            TWO_RIGHT: (two.at[unit, LOW], from_two_left.at[unit], RIGHT),
            TWO_LEFT: (two.at[unit, HIGH], from_two_right.at[unit], LEFT),
            RIGHT_HIGH: (to_right.at[unit, HIGH], from_left.at[unit, HIGH], RIGHT),
            LEFT_LOW: (to_left.at[unit, LOW], from_right.at[unit, LOW], LEFT),
            RIGHT_LOW: (to_right.at[unit, LOW], from_left.at[unit, LOW], RIGHT),
            LEFT_HIGH: (to_left.at[unit, HIGH], from_right.at[unit, HIGH], LEFT),
        }[kind]
        return remote(src, dst, sum_send.at[unit, kind], sum_recv.at[unit, kind], line[role])

    lane = lax.broadcasted_iota(jnp.int32, (PATCHES, 128), 1)
    mirror = {OPP: OPP, RIGHT: LEFT, LEFT: RIGHT}

    def stat_copies(image):
        return [
            remote(
                stats.at[image], stats_in.at[image, mirror[role]], stat_send.at[image, role],
                stat_recv.at[image, mirror[role]], line[role],
            )
            for role in (OPP, RIGHT, LEFT)
        ]

    def add_up(image):
        x_copies[image].wait()
        xf = x_ref[rows_of[image], :].astype(F32)
        sums = jnp.sum(xf, axis=-1, keepdims=True)
        both = jnp.where(lane == 0, sums, jnp.sum(xf * xf, axis=-1, keepdims=True))
        stats[image] = jnp.transpose(both)[0:8, :]
        return xf, sums

    for copy in small_copies:
        copy.wait()
    gain = gain_ref[...].reshape(1, BLOCK)
    xf, sums = add_up(0)
    lead[pl.ds(0, PATCHES), :] = ((xf - sums * (1.0 / BLOCK)) * gain).astype(BF16)
    high = gain.astype(BF16).astype(F32)
    line_at = lax.broadcasted_iota(jnp.int32, (16, BLOCK), 0)
    lead[pl.ds(PATCHES, 16), :] = jnp.where(
        line_at == 0, high, jnp.where(line_at == 1, gain - high, 0.0)
    ).astype(BF16)

    first_unit = 2 * SLOTS * gy

    def lead_product(role):
        full = jnp.dot(lead[...], wq[role, 0], preferred_element_type=F32)
        lead_out[role] = jnp.broadcast_to(
            full[PATCHES:PATCHES + 1, :] + full[PATCHES + 1:PATCHES + 2, :], (8, GROUP)
        )
        return full[0:PATCHES, :]

    lead_copies = [
        remote(
            lead_out.at[role], lead_in.at[mirror[role]], lead_send.at[role],
            lead_recv.at[mirror[role]], line[role],
        )
        for role in (OPP, RIGHT, LEFT)
    ]

    wait_weights(OPP, 0)
    two[first_unit] = lead_product(OPP).astype(BF16)
    for slot in range(SLOTS):
        for role in (OPP, RIGHT, LEFT, OWN):
            if slot != 0 or role == OWN:
                for copy in wq_copies(role, slot):
                    copy.start()

    pl.semaphore_wait(barrier, len(partners))

    for copy in stat_copies(0):
        copy.start()
    sum_copy(first_unit, TWO_RIGHT).start()
    sum_copy(first_unit, TWO_LEFT).start()
    wait_weights(RIGHT, 0)
    to_right[first_unit] = lead_product(RIGHT).astype(BF16)
    sum_copy(first_unit, RIGHT_HIGH).start()
    wait_weights(LEFT, 0)
    to_left[first_unit] = lead_product(LEFT).astype(BF16)
    sum_copy(first_unit, LEFT_LOW).start()
    add_up(1)
    for copy in stat_copies(1):
        copy.start()
    for copy in lead_copies:
        copy.start()

    def norm_copy(image):
        moved = normed.at[gy * 2 + image]
        return remote(moved, moved, norm_send.at[image], norm_recv.at[image], sibling)

    def normalize(image):
        for copy in stat_copies(image):
            copy.wait()
        shares = [stats_in[image, OPP], stats_in[image, RIGHT], stats_in[image, LEFT], stats[image]]
        total = shares[0] + shares[1] + shares[2] + shares[3]
        line_at = lax.broadcasted_iota(jnp.int32, (8, PATCHES), 0)
        part = jnp.where(line_at == 5, total[1:2, :], 0.0)
        for k, share in enumerate(shares + [total]):
            part = jnp.where(line_at == k, share[0:1, :], part)
        column = jnp.transpose(jnp.concatenate([part] * 16, axis=0))
        mean_value = column[:, 4:5] * (1.0 / D)
        spread = column[:, 5:6] * (1.0 / D) - mean_value * mean_value
        scale = lax.rsqrt(spread + EPS)
        if image == 0:
            fix[...] = jnp.where(lane == 4, scale, column * (1.0 / BLOCK) - mean_value)
        xf = x_ref[rows_of[image], :].astype(F32)
        normed[gy * 2 + image] = (
            (xf - mean_value) * scale * gain_ref[...].reshape(1, BLOCK)
        ).astype(BF16)
        norm_copy(image).start()

    def att_copy(unit, kind):
        every = pl.ds(0, PATCHES)
        rows, source, place, role = {
            ATT_RIGHT: (every, OWN, LEFT, RIGHT),
            ATT_LEFT: (every, OWN, RIGHT, LEFT),
            PASS_RIGHT: (LOW, LEFT, OPP, RIGHT),
            PASS_LEFT: (HIGH, RIGHT, OPP, LEFT),
        }[kind]
        return remote(
            attended.at[unit, rows, pl.ds(source * 128, 128)],
            attended.at[unit, rows, pl.ds(place * 128, 128)],
            att_send.at[unit, kind], att_recv.at[unit, kind], line[role],
        )

    def part_copy(image):
        return remote(
            leaving.at[image], other.at[image], part_send.at[image], part_recv.at[image], sibling
        )

    def first_copy(group, hop, step):
        to = lax.rem(last_at + step, RING)
        return remote(
            outgoing.at[group, hop - 1, to], middle.at[group, to, first_at],
            first_send.at[group, hop - 1, step], first_recv.at[group, hop - 1, step],
            (gx, gy, on_first(hop)),
        )

    columns = {core: pl.ds(core * WIDE, WIDE) for core in range(2)}

    def landing(core, source):
        if core == 0:
            return out_hbm.at[last_at, source, :, columns[core]]
        return out_hbm.at[source, last_at, :, columns[core]]

    def last_copy(group, hop, step, core):
        source = lax.rem(first_at + RING - hop, RING)
        return remote(
            middle.at[group, lax.rem(last_at + step, RING), source], landing(core, source),
            last_send.at[group, hop, step], last_recv.at[core, hop, step],
            (gx, group, on_last(step)),
        )

    def stay_copy(group, hop, core):
        source = lax.rem(first_at + RING - hop, RING)
        return pltpu.make_async_copy(
            middle.at[group, last_at, source], landing(core, source), local_sem.at[hop]
        )

    def product(unit, role):
        return jnp.dot(
            normed[lax.div(unit, SLOTS)], wq[role, lax.rem(unit, SLOTS)],
            preferred_element_type=F32,
        )

    def mend(values):
        for role in (OPP, RIGHT, LEFT):
            values = values + fix[:, role:role + 1] * lead_in[role][0:1, :]
        return fix[:, 4:5] * (values + fix[:, OWN:OWN + 1] * lead_out[OWN][0:1, :])

    def attend(unit, is_first):
        @pl.when(is_first)
        def _():
            held[...] = lead_product(OWN)
            for copy in lead_copies:
                copy.wait_recv()

        @pl.when(jnp.logical_not(is_first))
        def _():
            held[...] = product(unit, OWN)

        for kind in (RIGHT_HIGH, LEFT_LOW, RIGHT_LOW, LEFT_HIGH):
            sum_copy(unit, kind).wait_recv()
        held[...] += from_left[unit].astype(F32) + from_right[unit].astype(F32)

        @pl.when(is_first)
        def _():
            held[...] = mend(held[...])

        qkv = held[...]
        query = head_norm(qkv[:, 0:128], q_gain_ref[...])
        keys = head_norm(qkv[:, 128:256], k_gain_ref[...])
        values = qkv[:, 256:384].astype(BF16)
        scores = lax.dot_general(
            query, keys, (((1,), (1,)), ((), ())), preferred_element_type=F32
        ) * (1.0 / math.sqrt(128))
        expo = jnp.exp(scores)
        weights = (expo * (1.0 / jnp.sum(expo, axis=-1, keepdims=True))).astype(BF16)
        attended[unit, :, pl.ds(OWN * 128, 128)] = jnp.dot(
            weights, values, preferred_element_type=F32
        ).astype(BF16)
        att_copy(unit, ATT_RIGHT).start()
        att_copy(unit, ATT_LEFT).start()

    def project(image, side, slots):
        parts = [
            jnp.dot(attended[image * SLOTS + slot], wo[side, slot], preferred_element_type=F32)
            for slot in slots
        ]
        return parts[0] if len(parts) == 1 else parts[0] + parts[1]

    def send_last(group, hop, step):
        for core in range(2):
            @pl.when(gy == core)
            def _():
                if step != 0:
                    last_copy(group, hop, step, core).start()
                else:
                    @pl.when(group == gy)
                    def _():
                        stay_copy(group, hop, core).start()

                    @pl.when(group != gy)
                    def _():
                        last_copy(group, hop, 0, core).start()

    def route_on(group):
        for hop in (1, 3, 2):
            for step in (2, 1, 3):
                first_copy(group, hop, step).wait_recv()
                send_last(group, hop, step)
        for hop in range(1, RING):
            first_copy(group, hop, 0).wait_recv()
            send_last(group, hop, 0)

    def finish(held_image):
        part_copy(held_image).wait_recv()
        rows = pl.ds(pl.multiple_of(lax.rem(held_image, 2) * PATCHES, PATCHES), PATCHES)
        layer[rows, :] = (
            x_half[lax.div(held_image, 2), rows, :].astype(F32)
            + (mine[held_image].astype(F32) + other[held_image].astype(F32))
        ).astype(BF16)

    def prepare(group):
        finish(2 * group)
        place = lax.broadcasted_iota(jnp.int32, (RING * CAP, 1), 0)
        places = target[group][0:1, :]
        for step in range(RING):
            rank = plane(lax.rem(first_at + step, RING), place >> 6)
            picks[step] = jnp.where(
                rank * CAP + (place & (CAP - 1)) == places, 1.0, 0.0
            ).astype(BF16)
            even = jnp.dot(
                picks[step, :, 0:PATCHES], layer[0:PATCHES, :], preferred_element_type=F32
            ).astype(BF16).reshape(RING, CAP, WIDE)
            if step == 0:
                for to in range(RING):
                    middle[group, to, first_at] = even[to]
            else:
                outgoing[group, step - 1] = even

    def route(group):
        finish(2 * group + 1)
        for step in (1, 3, 2, 0):
            picked = jnp.dot(
                picks[step, :, PATCHES:], layer[PATCHES:, :], preferred_element_type=F32
            ).reshape(RING, CAP, WIDE)
            if step == 0:
                for to in range(RING):
                    middle[group, to, first_at] = (
                        middle[group, to, first_at].astype(F32) + picked[to]
                    ).astype(BF16)
            else:
                outgoing[group, step - 1] = (
                    outgoing[group, step - 1].astype(F32) + picked
                ).astype(BF16)
                for on in (2, 1, 3):
                    first_copy(group, step, on).start()
        for step in (1, 3, 2):
            first_copy(group, step, 0).start()
        for on in (2, 1, 3, 0):
            send_last(group, 0, on)

    def towards_opposite(unit):
        two[unit] = product(unit, OPP).astype(BF16)
        sum_copy(unit, TWO_RIGHT).start()
        sum_copy(unit, TWO_LEFT).start()

    normalize(0)
    sum_copy(first_unit, TWO_RIGHT).wait_recv()
    to_right[first_unit, LOW, :] = (
        to_right[first_unit, LOW, :].astype(F32) + from_two_left[first_unit].astype(F32)
    ).astype(BF16)
    sum_copy(first_unit, RIGHT_LOW).start()
    sum_copy(first_unit, TWO_LEFT).wait_recv()
    to_left[first_unit, HIGH, :] = (
        to_left[first_unit, HIGH, :].astype(F32) + from_two_right[first_unit].astype(F32)
    ).astype(BF16)
    sum_copy(first_unit, LEFT_HIGH).start()
    wait_weights(OPP, 1)

    @pl.when(gy == 0)
    def _():
        towards_opposite(1)

    normalize(1)

    @pl.when(gy == 1)
    def _():
        norm_copy(0).wait_recv()
        towards_opposite(0)

    row = lax.broadcasted_iota(jnp.int32, (8, 2 * PATCHES), 1)
    places = jnp.full((8, 2 * PATCHES), RANKS * CAP, jnp.int32)
    for image in range(2):
        begin = image * PATCHES
        for piece in range(8):
            stop = begin + counts_ref[image, piece]
            places = jnp.where(
                (row >= begin) & (row < stop), dest_ref[image, piece] * CAP + row - begin, places
            )
            begin = stop
    target[gy] = places
    target_copy = remote(target.at[gy], target.at[gy], target_send, target_recv, sibling)
    target_copy.start()
    cross_copy = remote(
        x_hbm.at[:, pl.ds(pl.multiple_of((1 - gy) * WIDE, WIDE), WIDE)],
        x_half.at[gy], half_send, half_recv, sibling,
    )
    cross_copy.start()
    half_copy.start()
    for copy in wo_copies():
        copy.start()

    def turn(step, carry):
        def back(count):
            at_turn = lax.rem(step + UNITS - count, UNITS)
            late = lax.div(at_turn, 2 * SLOTS + 1)
            shifted = lax.rem(at_turn + 2 * SLOTS, 2 * SLOTS + 1)
            return (1 - gy) * at_turn + gy * (late * at_turn + (1 - late) * shifted)

        @pl.when((step == 9) | (step == 14))
        def _():
            prepare(lax.div(step, 14))

        @pl.when((step >= 2) & (step <= UNITS))
        def _():
            unit = back(1)

            @pl.when(step <= SLOTS)
            def _():
                wait_weights(RIGHT, lax.rem(step + 2, SLOTS))
                wait_weights(LEFT, lax.rem(step + 2, SLOTS))

            mine_right = product(unit, RIGHT)
            to_right[unit, HIGH, :] = mine_right[HALF:, :].astype(BF16)
            sum_copy(unit, RIGHT_HIGH).start()
            sum_copy(unit, TWO_RIGHT).wait_recv()
            to_right[unit, LOW, :] = (
                mine_right[:HALF, :] + from_two_left[unit].astype(F32)
            ).astype(BF16)
            sum_copy(unit, RIGHT_LOW).start()
            mine_left = product(unit, LEFT)
            to_left[unit, LOW, :] = mine_left[:HALF, :].astype(BF16)
            sum_copy(unit, LEFT_LOW).start()
            sum_copy(unit, TWO_LEFT).wait_recv()
            to_left[unit, HIGH, :] = (
                mine_left[HALF:, :] + from_two_right[unit].astype(F32)
            ).astype(BF16)
            sum_copy(unit, LEFT_HIGH).start()

        @pl.when((step >= 1) & (step <= UNITS - 2))
        def _():
            unit = back(-1)
            image = lax.div(unit, SLOTS)

            @pl.when((lax.rem(unit, SLOTS) == 0) & (lax.div(image, 2) != gy))
            def _():
                norm_copy(lax.rem(image, 2)).wait_recv()

            @pl.when(step == 1)
            def _():
                wait_weights(OPP, 2)

            towards_opposite(unit)

        @pl.when((step >= 2) & (step <= UNITS + 1))
        def _():
            unit = back(2)

            @pl.when(step < SLOTS + 2)
            def _():
                wait_weights(OWN, lax.rem(step + 1, SLOTS))

            attend(unit, step == 2)

        @pl.when((step >= 3) & (step <= UNITS + 2))
        def _():
            unit = back(3)
            att_copy(unit, ATT_RIGHT).wait_recv()
            att_copy(unit, PASS_RIGHT).start()
            att_copy(unit, ATT_LEFT).wait_recv()
            att_copy(unit, PASS_LEFT).start()

        @pl.when((step == 7) | (step == 10) | (step == 13) | (step == 16))
        def _():
            image = lax.div(step, 3) - 2

            @pl.when(step == 7)
            def _():
                for copy in wo_copies():
                    copy.wait()
                half_copy.wait()
                target_copy.wait()
                cross_copy.wait()

            def wait_slot(slot):
                att_copy(image * SLOTS + slot, PASS_RIGHT).wait_recv()
                att_copy(image * SLOTS + slot, PASS_LEFT).wait_recv()

            wait_slot(0)
            wait_slot(1)
            early = [project(image, side, (0, 1)) for side in range(2)]
            wait_slot(2)
            leaving[image] = (early[0] + project(image, 0, (2,))).astype(BF16)
            part_copy(image).start()
            mine[image] = (early[1] + project(image, 1, (2,))).astype(BF16)

        @pl.when((step == 10) | (step == 16))
        def _():
            route(lax.div(step, 16))

        @pl.when((step == 12) | (step == 17))
        def _():
            route_on(lax.div(step, 17))

        return carry

    lax.fori_loop(1, UNITS + 6, turn, 0)

    def drain(unit, carry):
        for kind in range(6):
            sum_copy(unit, kind).wait_send()
        for kind in range(4):
            att_copy(unit, kind).wait_send()
        return carry

    lax.fori_loop(0, UNITS, drain, 0)
    for copy in lead_copies:
        copy.wait_send()
    for image in range(2):
        norm_copy(image).wait_send()
    for image in range(IMAGES):
        part_copy(image).wait_send()
    for group in range(2):
        for hop in range(1, RING):
            for step in range(RING):
                first_copy(group, hop, step).wait_send()
        for hop in range(RING):
            for step in range(1, RING):
                last_copy(group, hop, step, group).wait_send()
                last_copy(group, hop, step, group).wait_recv()

            @pl.when(group != gy)
            def _():
                last_copy(group, hop, 0, group).wait_send()
                last_copy(group, hop, 0, group).wait_recv()

            @pl.when(group == gy)
            def _():
                stay_copy(group, hop, group).wait()


def on_device(x_in, ln_gain, w_qkv, q_gain, k_gain, w_out, counts, dest):
    any_spec = pl.BlockSpec(memory_space=pl.ANY)
    dma = pltpu.SemaphoreType.DMA
    routed = pl.pallas_call(
        kernel,
        out_shape=pltpu.VMEM((RING, RING, CAP, BLOCK), BF16),
        in_specs=[any_spec] * 8,
        out_specs=any_spec,
        scratch_shapes=[
            pltpu.VMEM((2 * PATCHES, BLOCK), BF16),
            pltpu.VMEM((BLOCK,), F32),
            pltpu.VMEM((1, 128), F32),
            pltpu.VMEM((1, 128), F32),
            pltpu.SMEM((2, 8), jnp.int32),
            pltpu.SMEM((2, 8), jnp.int32),
            pltpu.VMEM((2, 2 * PATCHES, WIDE), BF16),
            pltpu.VMEM((IMAGES, PATCHES, BLOCK), BF16),
            pltpu.VMEM((4, SLOTS, BLOCK, GROUP), BF16),
            pltpu.VMEM((2, SLOTS, 4 * 128, WIDE), BF16),
            pltpu.VMEM((UNITS, PATCHES, GROUP), BF16),
            pltpu.VMEM((UNITS, PATCHES, GROUP), BF16),
            pltpu.VMEM((UNITS, PATCHES, GROUP), BF16),
            pltpu.VMEM((UNITS, HALF, GROUP), BF16),
            pltpu.VMEM((UNITS, HALF, GROUP), BF16),
            pltpu.VMEM((UNITS, PATCHES, GROUP), BF16),
            pltpu.VMEM((UNITS, PATCHES, GROUP), BF16),
            pltpu.VMEM((UNITS, PATCHES, 4 * 128), BF16),
            pltpu.VMEM((PATCHES, GROUP), F32),
            pltpu.VMEM((PATCHES + 16, BLOCK), BF16),
            pltpu.VMEM((PATCHES, 128), F32),
            pltpu.VMEM((4, 8, GROUP), F32),
            pltpu.VMEM((3, 8, GROUP), F32),
            pltpu.VMEM((IMAGES, PATCHES, WIDE), BF16),
            pltpu.VMEM((IMAGES, PATCHES, WIDE), BF16),
            pltpu.VMEM((IMAGES, PATCHES, WIDE), BF16),
            pltpu.VMEM((2 * PATCHES, WIDE), BF16),
            pltpu.VMEM((RING, RING * CAP, 2 * PATCHES), BF16),
            pltpu.VMEM((2, RING - 1, RING, CAP, WIDE), BF16),
            pltpu.VMEM((2, RING, RING, CAP, WIDE), BF16),
            pltpu.VMEM((2, 8, 2 * PATCHES), jnp.int32),
            pltpu.VMEM((2, 8, PATCHES), F32),
            pltpu.VMEM((2, 3, 8, PATCHES), F32),
            dma((2,)),
            dma((5,)),
            dma(()),
            dma((4, SLOTS, 3)),
            dma((2, SLOTS, 4)),
            dma(()),
            dma(()),
            dma(()),
            dma(()),
            dma((2, 3)),
            dma((2, 3)),
            dma((3,)),
            dma((3,)),
            dma((2,)),
            dma((2,)),
            dma((UNITS, 6)),
            dma((UNITS, 6)),
            dma((UNITS, 4)),
            dma((UNITS, 4)),
            dma((IMAGES,)),
            dma((IMAGES,)),
            dma((2, RING - 1, RING)),
            dma((2, RING - 1, RING)),
            dma((2, RING, RING)),
            dma((2, RING, RING)),
            dma((RING,)),
        ],
        compiler_params=pltpu.CompilerParams(
            collective_id=0, has_side_effects=True, vmem_limit_bytes=58 * 2**20
        ),
        cost_estimate=pl.CostEstimate(
            flops=20 * 10**9, bytes_accessed=25 * 10**6, transcendentals=10**6
        ),
        name="layer",
    )(
        x_in.reshape(2 * PATCHES, BLOCK),
        ln_gain,
        jnp.transpose(w_qkv, (1, 2, 0, 3)),
        q_gain.reshape(1, 128),
        k_gain.reshape(1, 128),
        w_out.reshape(BLOCK, BLOCK),
        counts,
        dest,
    )
    return routed.reshape(1, 1, RANKS, 1, CAP, BLOCK)


def solution(mesh):
    in_specs = (
        P(("gy", "gz"), None, "gx"),
        P("gx"),
        P("gx", "gy", None, None),
        P(),
        P(),
        P("gy", None, "gx"),
        P(("gy", "gz"), None),
        P(("gy", "gz"), None),
    )
    out_specs = P("gy", "gz", None, None, None, "gx")
    return jax.shard_map(
        on_device, mesh=mesh, in_specs=in_specs, out_specs=out_specs, check_vma=False
    )
```
